256 devices in a mesh: seq: 32 (over z, y_lo, core), fsdp: 8 (over y_hi, x).
Axes of the slice: x: 4, y: 4 (y_hi: 2, y_lo: 2; y = y_hi * 2 + y_lo), z: 8, core: 2. Of those that a mesh axis runs over, the one named last changes fastest.
Arguments:
- hidden: bfloat16 [8, 4096, 2048], P('fsdp', 'seq'), may hold values from -6 to 6
- tokens: int32 [8, 4096], P('fsdp', 'seq'), may hold values from 0 to 4
- base_bias: bfloat16 [5, 2048], replicated, may hold values from -3 to 3
- in_weight: bfloat16 [1024, 4384], P('fsdp'), may hold values from -0.1875 to 0.1875
- conv_weight: float32 [4, 2304], replicated, may hold values from -3 to 3
- conv_bias: float32 [2304], replicated, may hold values from -2 to 2
- dt_bias: float32 [32], replicated, may hold values from -1 to 1
- decay_rate: float32 [32], replicated, may hold values from 7.3242186e-06 to 0.04
- norm_gain: float32 [2048], replicated, may hold values from 0.1 to 1.9
- out_weight: bfloat16 [2048, 1024], P('fsdp'), may hold values from -0.125 to 0.125
Outputs:
- mixed: bfloat16 [8, 4096, 2048], P('fsdp', 'seq')
The draws below stay inside these ranges and needn't reach their ends.
Inputs may be any that keep to these rules, and one draw needn't show every extreme that they name: `tokens`: 0 to 3 are the bases A, C, G, T and 4 is an unknown base.
All inputs are finite; a program needn't handle non-finite values.
Results may differ from the reference program's by a relative error of at most 0.0069.
Values may be sent and summed in bfloat16 or wider, within the bound.
No kernel may reach another device: no remote copies, remote signals or barrier semaphores. Data moves between devices by JAX's collectives and lax.ppermute only.
A program may use at most 256 MiB of HBM per device.

```python
import math
import jax
import jax.numpy as jnp
from jax import lax

D = 1024
HEADS = 32
HEADDIM = 64
STATE = 128
CONV = 4
GROUP = 128
E = 2048
WIDE = 4384
LENGTH = 4096
SLABS = 8


def touch_ends(entries, stream_key, least, high):
    longest = entries.shape.index(max(entries.shape))
    spots = []
    for shift in (0, 1):
        where = [jax.random.randint(jax.random.fold_in(stream_key, axis), (), 0, length) for axis, length in enumerate(entries.shape)]
        where[longest] = (where[longest] + shift) % entries.shape[longest]
        spots.append(tuple(where))
    return entries.at[spots[0]].set(least).at[spots[1]].set(high)


def shard_levels(rng, extent, split, low, high):
    factor_of = 1.0
    for dim, parts in split:
        draws = jax.random.uniform(jax.random.fold_in(jax.random.fold_in(rng, 6), dim), (parts,), jnp.float32, low / len(split), high / len(split))
        factor_of = factor_of * jnp.repeat(jnp.exp(draws), extent[dim] // parts).reshape((-1,) + (1,) * (len(extent) - 1 - dim))
    return factor_of


def normal_values(stream_key, dims, width, reach, cuts=(), kind=jnp.bfloat16):
    factor_of = shard_levels(stream_key, dims, cuts, -0.22, 0.18) if cuts else 1.0
    entries = jax.random.normal(stream_key, dims, jnp.float32) * width * factor_of
    return jnp.minimum(jnp.maximum(entries, -reach), reach).astype(kind)


def setup_inputs(seed: int = 0) -> dict:
    keys = jax.random.split(jax.random.key(seed), 11)
    hidden = normal_values(keys[0], (SLABS, LENGTH, 2 * D), 1.0, 6.0, ((0, 8), (1, 32)))
    tokens = touch_ends(jax.random.randint(keys[1], (SLABS, LENGTH), 0, 5), jax.random.fold_in(keys[1], 1), 0, 4).astype(jnp.int32)
    base_bias = normal_values(keys[2], (5, 2 * D), 0.5, 3.0)
    in_weight = normal_values(keys[3], (D, WIDE), D ** -0.5, 0.1875, ((0, 8),))
    conv_weight = normal_values(keys[4], (CONV, E + 2 * STATE), 0.5, 3.0, (), jnp.float32)
    conv_bias = normal_values(keys[5], (E + 2 * STATE,), 0.3, 2.0, (), jnp.float32)
    dt_bias = jnp.clip(jax.random.uniform(keys[6], (HEADS,), jnp.float32, -1.0, 1.0), -1.0, 1.0)
    decay_rate = jnp.clip(jnp.exp(jax.random.uniform(keys[7], (HEADS,), jnp.float32, math.log(7.324218586290954e-06), math.log(0.04))), 7.324218586290954e-06, 0.04)
    norm_gain = jnp.clip(1.0 + 0.18 * jax.random.normal(keys[8], (E,), jnp.float32), 0.1, 1.9)
    out_weight = normal_values(keys[9], (E, D), E ** -0.5, 0.125, ((0, 8),))
    return dict(hidden=hidden, tokens=tokens, base_bias=base_bias, in_weight=in_weight, conv_weight=conv_weight, conv_bias=conv_bias, dt_bias=dt_bias, decay_rate=decay_rate, norm_gain=norm_gain, out_weight=out_weight)


def group_pass(carried, pieces, rates):
    values, in_map, out_map, step_size = pieces
    span = values.shape[0]
    log_decay = -step_size * rates[None, :]
    cumulated = jnp.cumsum(log_decay, axis=0)
    position = jnp.arange(span)
    causal = position[:, None] >= position[None, :]
    log_gap = jnp.where(causal[:, :, None], cumulated[:, None, :] - cumulated[None, :, :], -1e+30)
    affinity = jnp.dot(out_map.astype(jnp.bfloat16), in_map.astype(jnp.bfloat16).T, preferred_element_type=jnp.float32)
    mixing = affinity[:, :, None] * jnp.exp(log_gap) * step_size[None, :, :]
    within = jnp.einsum('tsh,shp->thp', mixing, values, precision=lax.Precision.HIGHEST)
    entering_part = jnp.einsum('tn,hpn->thp', out_map, carried, precision=lax.Precision.HIGHEST) * jnp.exp(cumulated)[:, :, None]
    remaining = jnp.exp(cumulated[-1][None, :] - cumulated) * step_size
    updated = carried * jnp.exp(cumulated[-1])[:, None, None] + jnp.einsum('sh,shp,sn->hpn', remaining, values, in_map, precision=lax.Precision.HIGHEST)
    return (updated, within + entering_part)

def prepare(projected, preceding, conv_weight, conv_bias, dt_bias):
    row_count = projected.shape[0]
    gate_part = projected[:, :E].astype(jnp.float32)
    conv_input = projected[:, E:2 * E + 2 * STATE]
    padded = jnp.concatenate([preceding, conv_input], axis=0).astype(jnp.float32)
    convolved = jnp.zeros((row_count, E + 2 * STATE), jnp.float32) + conv_bias[None, :]
    for offset in range(CONV):
        convolved = convolved + conv_weight[offset][None, :] * padded[offset:offset + row_count]
    activated = lax.optimization_barrier(jax.nn.silu(convolved).astype(jnp.bfloat16)).astype(jnp.float32)
    values = activated[:, :E].reshape(row_count, HEADS, HEADDIM)
    in_map = activated[:, E:E + STATE]
    out_map = activated[:, E + STATE:]
    step_size = jax.nn.softplus(projected[:, 2 * E + 2 * STATE:].astype(jnp.float32) + dt_bias[None, :])
    return (values, in_map, out_map, step_size, gate_part)

def finish(outputs, gate_part, norm_gain):
    row_count = outputs.shape[0]
    full = outputs.reshape(row_count, E)
    gated = full * jax.nn.silu(gate_part)
    scale = lax.rsqrt(lax.optimization_barrier(jnp.mean(gated * gated, axis=-1, keepdims=True)) + 1e-05)
    return (gated * scale * norm_gain[None, :]).astype(jnp.bfloat16)

def strand_mixer(source, in_weight, conv_weight, conv_bias, dt_bias, decay_rate, norm_gain, out_weight):
    projected = lax.optimization_barrier(jnp.dot(source, in_weight, preferred_element_type=jnp.float32).astype(jnp.bfloat16))
    preceding = jnp.zeros((CONV - 1, E + 2 * STATE), jnp.bfloat16)
    values, in_map, out_map, step_size, gate_part = prepare(projected, preceding, conv_weight, conv_bias, dt_bias)
    count = LENGTH // GROUP
    pieces = (values.reshape(count, GROUP, HEADS, HEADDIM), in_map.reshape(count, GROUP, STATE), out_map.reshape(count, GROUP, STATE), step_size.reshape(count, GROUP, HEADS))
    start_state = jnp.zeros((HEADS, HEADDIM, STATE), jnp.float32)
    final_state, outputs = lax.scan(lambda carried, piece: group_pass(carried, piece, decay_rate), start_state, pieces)
    outputs = outputs.reshape(LENGTH, HEADS, HEADDIM)
    normed = finish(outputs, gate_part, norm_gain)
    return jnp.dot(normed, out_weight, preferred_element_type=jnp.float32).astype(jnp.bfloat16)

def reference(hidden, tokens, base_bias, in_weight, conv_weight, conv_bias, dt_bias, decay_rate, norm_gain, out_weight):

    def one_slab(pair):
        rows_in, base_ids = pair
        paired = jnp.where(base_ids == 4, 4, 3 - base_ids).astype(jnp.int32)
        forward_input = (rows_in[:, :D].astype(jnp.float32) + base_bias[base_ids][:, :D].astype(jnp.float32)).astype(jnp.bfloat16)
        reverse_rows = (rows_in[:, D:].astype(jnp.float32) + base_bias[paired][:, D:].astype(jnp.float32)).astype(jnp.bfloat16)
        reverse_input = jnp.flip(jnp.flip(reverse_rows, axis=0), axis=1)
        forward_out = strand_mixer(forward_input, in_weight, conv_weight, conv_bias, dt_bias, decay_rate, norm_gain, out_weight)
        reverse_out = strand_mixer(reverse_input, in_weight, conv_weight, conv_bias, dt_bias, decay_rate, norm_gain, out_weight)
        return jnp.concatenate([forward_out, jnp.flip(jnp.flip(reverse_out, axis=0), axis=1)], axis=1)
    return lax.map(one_slab, (hidden, tokens))
```

```python
import jax
import jax.numpy as jnp
from jax import lax
from jax.experimental import pallas as pl
from jax.experimental.pallas import tpu as pltpu
from jax.sharding import PartitionSpec as P

D = 1024
HEADS = 32
HEADDIM = 64
STATE = 128
CONV = 4
GROUP = 128
E = 2048
WIDE = 4384
ROWS = 128
SPAN = 512
OWN = 512
HALO = 16
PAD = HALO + SPAN
WA = OWN + 2 * STATE + 128
Z = 8

F32 = jnp.float32
BF16 = jnp.bfloat16
EXACT = lax.Precision.HIGHEST
ANY = pl.BlockSpec(memory_space=pl.ANY)
VMEM = pl.BlockSpec(memory_space=pltpu.VMEM)


def place():
    s, f = lax.axis_index("seq"), lax.axis_index("fsdp")
    t = lax.rem(s, 4)
    return s // 4, t // 2, lax.rem(t, 2), f // 4, lax.rem(f, 4), t


def move(value, to):
    pairs = []
    for s in range(32):
        for f in range(8):
            here = dict(z=s // 4, yl=(s // 2) % 2, c=s % 2, yh=f // 4, x=f % 4)
            change = to(**here)
            if change is None:
                continue
            there = {**here, **change}
            target = (there["z"] * 4 + there["yl"] * 2 + there["c"]) * 8 + there["yh"] * 4 + there["x"]
            pairs.append((s * 8 + f, target))
    return lax.ppermute(value, ("seq", "fsdp"), pairs)


def params(mb, flops=0, bytes_accessed=0):
    return dict(
        compiler_params=pltpu.CompilerParams(vmem_limit_bytes=mb << 20),
        cost_estimate=pl.CostEstimate(flops=flops, bytes_accessed=bytes_accessed, transcendentals=0),
    )


def iota2(shape, dim):
    return lax.broadcasted_iota(jnp.int32, shape, dim)


def ones_at(where):
    return jnp.where(where, 1.0, 0.0)


def anti_identity():
    return ones_at(iota2((128, 128), 0) + iota2((128, 128), 1) == 127).astype(BF16)


def flipped(block):
    anti = anti_identity()
    rows = jnp.dot(anti, block, preferred_element_type=F32).astype(BF16)
    parts = [
        jnp.dot(rows[:, 128 * j : 128 * j + 128], anti, preferred_element_type=F32).astype(BF16)
        for j in range(D // 128)
    ]
    return jnp.concatenate(parts[::-1], axis=1)


def pack_weights(iw, ow, cw, cb, dtb, rate, gain, ua, ua_other, ub, ub_other, prm, stack):
    _, yl, c, _, _, t = place()
    t_other = (1 - yl) * 2 + c
    row, col = iota2((512, 256), 0), iota2((512, 256), 1)
    inner = lax.rem(col, 128)
    head = jnp.where(col < 128, t, t_other)
    pick = ones_at(row == 256 * (inner // 64) + 64 * head + lax.rem(inner, 64))
    pick_bf = pick.astype(BF16)
    for j in range(4):
        got = jnp.dot(iw[:, E + 512 * j : E + 512 * j + 512], pick_bf, preferred_element_type=F32).astype(BF16)
        ua[:, 128 * j : 128 * j + 128] = got[:, :128]
        ua_other[:, 128 * j : 128 * j + 128] = got[:, 128:]
        got = jnp.dot(iw[:, 512 * j : 512 * j + 512], pick_bf, preferred_element_type=F32).astype(BF16)
        ub[:128, 128 * j : 128 * j + 128] = got[:, :128]
        ub_other[:128, 128 * j : 128 * j + 128] = got[:, 128:]
    both = iw[:, 2 * E : 2 * E + 2 * STATE]
    ua[:, OWN : OWN + 2 * STATE] = both
    ua_other[:, OWN : OWN + 2 * STATE] = both
    lane, out = iota2((HEADS, 256), 0), iota2((HEADS, 256), 1)
    inner = lax.rem(out, 128)
    step_pick = ones_at((lane == 4 * inner + jnp.where(out < 128, t, t_other)) & (inner < 8))
    got = jnp.dot(iw[:, 2 * E + 2 * STATE :], step_pick.astype(BF16), preferred_element_type=F32).astype(BF16)
    ua[:, OWN + 2 * STATE :] = got[:, :128]
    ua_other[:, OWN + 2 * STATE :] = got[:, 128:]
    for ref, which in ((ub, t), (ub_other, t_other)):
        rows = ow[pl.ds(pl.multiple_of(64 * which, 64), 64), :]
        ref[128:192, :] = rows[:, :512]
        ref[192:256, :] = rows[:, 512:]
    stack[...] = jnp.zeros_like(stack)
    stack[0:4, :] = cw[:, :E]
    stack[4:5, :] = cb[:, :E]
    stack[5:6, :] = gain[...]
    prm[...] = jnp.zeros_like(prm)
    for j in range(4):
        prm[:, 128 * j : 128 * j + 128] = jnp.dot(
            stack[:, 512 * j : 512 * j + 512], pick[:, :128], precision=EXACT, preferred_element_type=F32
        )
    prm[0:4, OWN : OWN + 2 * STATE] = cw[:, E:]
    prm[4:5, OWN : OWN + 2 * STATE] = cb[:, E:]
    stack[0:1, :HEADS] = dtb[...]
    stack[1:2, :HEADS] = rate[...]
    prm[:, OWN + 2 * STATE :] = jnp.dot(
        stack[:, :HEADS], step_pick[:, :128], precision=EXACT, preferred_element_type=F32
    )


def prepare_inputs(hidden, tokens, base_bias, act, halo):
    _, _, c, _, _, _ = place()
    ids = tokens[...]
    letter = iota2((8, ROWS), 0)
    paired = jnp.where(ids == 4, 4, 3 - ids)
    for strand, chosen in ((0, ids), (1, paired)):
        onehot = ones_at(letter == chosen).astype(BF16)
        bias = lax.dot_general(
            onehot, base_bias[:, D * strand : D * strand + D], (((0,), (0,)), ((), ())), preferred_element_type=F32
        )
        block = (hidden[:, D * strand : D * strand + D].astype(F32) + bias).astype(BF16)
        if strand:
            block = flipped(block)
        act[ROWS * strand : ROWS * strand + ROWS, :] = block
    halo[...] = jnp.where(c == 1, act[ROWS - HALO : ROWS, :], act[2 * ROWS - HALO :, :])


def fetch(copies):
    for copy in copies:
        copy.start()
    for copy in copies:
        copy.wait()


def weight_rows():
    _, _, _, yh, x, _ = place()
    return [which * 4 + lax.rem(x - k + 4, 4) for which in (yh, 1 - yh) for k in range(4)]


def act_copies(blocks, act, sems):
    _, _, _, _, _, t = place()
    copies = []
    for n, (block, other) in enumerate(zip(blocks, (0, 2, 1, 3))):
        at = t ^ other
        for strand, row in ((0, at), (1, 3 - at)):
            copies.append(
                pltpu.make_async_copy(
                    block.at[pl.ds(ROWS * strand, ROWS)],
                    act.at[strand, pl.ds(pl.multiple_of(HALO + ROWS * row, 16), ROWS)],
                    sems.at[2 * n + strand],
                )
            )
    return copies


def spread():
    return ones_at(iota2((128, OWN), 0) == iota2((128, OWN), 1) // HEADDIM)


def lower():
    return ones_at(iota2((GROUP, GROUP), 0) >= iota2((GROUP, GROUP), 1))


def exact_dot(a, b):
    return jnp.dot(a, b, precision=EXACT, preferred_element_type=F32)


def hi_lo(v):
    hi = v.astype(BF16).astype(F32)
    return hi, v - hi


def scan_kernel(*refs):
    blocks, refs = refs[:4], refs[4:]
    halos, refs = refs[:3], refs[3:]
    units, refs = refs[:8], refs[8:]
    prm, refs = refs[0], refs[1:]
    xs, maps, step, starts, *sends = refs[:11]
    act, halo, weight, proj, ends, asem, hsem, wsem, ssem = refs[11:]
    z, _, c, _, _, _ = place()
    copies = act_copies(blocks, act, asem)
    copies += [pltpu.make_async_copy(h, halo.at[n], hsem.at[n]) for n, h in enumerate(halos)]
    for n, (unit, f) in enumerate(zip(units, weight_rows())):
        rows = pl.ds(pl.multiple_of(128 * f, 128), 128)
        copies.append(pltpu.make_async_copy(unit, weight.at[rows], wsem.at[n]))
    fetch(copies)
    near = halo[0] + halo[1]
    far = halo[2]
    act[0, :HALO, :] = jnp.where(c == 1, near, far)
    act[1, :HALO, :] = jnp.where(c == 1, far, near)
    expand = spread()
    triangle = lower()

    def one_strand(strand, _):
        proj[...] = jnp.dot(act[strand], weight[...], preferred_element_type=F32).astype(BF16).astype(F32)
        for j in range(6):
            cols = slice(128 * j, 128 * j + 128)
            acc = prm[4:5, cols] + prm[0:1, cols] * proj[HALO - 3 : HALO - 3 + SPAN, cols]
            for k in range(1, CONV):
                acc = acc + prm[k : k + 1, cols] * proj[HALO - 3 + k : HALO - 3 + k + SPAN, cols]
            half = 0.5 * acc
            done = (half + half * jnp.tanh(half)).astype(BF16)
            if j < 4:
                xs[strand, :, cols] = done
            else:
                maps[strand, :, 128 * (j - 4) : 128 * (j - 4) + 128] = done
        raw = proj[HALO:, OWN + 2 * STATE :] + prm[0:1, OWN + 2 * STATE :]
        size = jnp.maximum(raw, 0.0) + jnp.log1p(jnp.exp(-jnp.abs(raw)))
        step[strand] = size
        decay = -size * prm[1:2, OWN + 2 * STATE :]
        state = jnp.zeros((STATE, OWN), F32)
        total = jnp.zeros((1, 128), F32)
        for g in range(SPAN // GROUP):
            rows = slice(GROUP * g, GROUP * g + GROUP)
            cumulated = exact_dot(triangle, decay[rows])
            last = cumulated[GROUP - 1 :, :]
            total = total + last
            remaining = exact_dot(jnp.exp(last - cumulated) * size[rows], expand)
            weighted = (xs[strand, rows, :].astype(F32) * remaining).astype(BF16)
            starts[strand, g] = state.astype(BF16)
            added = lax.dot_general(
                maps[strand, rows, :STATE], weighted, (((0,), (0,)), ((), ())), preferred_element_type=F32
            )
            kept = exact_dot(jnp.broadcast_to(jnp.exp(last), (8, 128)), expand)[0:1]
            state = state * kept + added
        ends[strand, :STATE, :] = state.astype(BF16)
        hi, lo = hi_lo(exact_dot(jnp.broadcast_to(total, (8, 128)), expand))
        line = iota2((HALO, OWN), 0)
        ends[strand, STATE:, :] = jnp.where(line == 0, hi[0:1], jnp.where(line == 1, lo[0:1], 0.0)).astype(BF16)
        return 0

    lax.fori_loop(0, 2, one_strand, 0)
    out = []
    for k in range(1, Z):
        strand = jnp.where(z + k < Z, 0, 1)
        out.append(pltpu.make_async_copy(ends.at[strand], sends[k - 1], ssem.at[k - 1]))
    fetch(out)


def local_kernel(*refs):
    blocks, refs = refs[:4], refs[4:]
    units, refs = refs[:8], refs[8:]
    prm, xs, maps, step, starts, local, carry, act, weight, asem, wsem = refs
    copies = act_copies(blocks, act, asem)
    for n, (unit, f) in enumerate(zip(units, weight_rows())):
        rows = pl.ds(pl.multiple_of(128 * f, 128), 128)
        copies.append(pltpu.make_async_copy(unit.at[pl.ds(0, 128)], weight.at[rows], wsem.at[n]))
    fetch(copies)
    expand = spread()
    triangle = lower()
    left = iota2((GROUP, 128), 1) < HEADDIM

    def one_strand(strand, _):
        rates = prm[1:2, OWN + 2 * STATE :]

        def one_group(g, before):
            at = pl.multiple_of(GROUP * g, GROUP)
            rows = pl.ds(at, GROUP)
            gate = jnp.dot(
                act[strand, pl.ds(pl.multiple_of(HALO + at, 16), GROUP), :], weight[...], preferred_element_type=F32
            )
            half = 0.5 * gate.astype(BF16).astype(F32)
            gate = half + half * jnp.tanh(half)
            size = step[strand, rows, :]
            cumulated = exact_dot(triangle, -size * rates)
            turned = cumulated.T
            size_turned = size.T
            in_map = maps[strand, rows, :STATE]
            out_map = maps[strand, rows, STATE:]
            affinity = lax.dot_general(
                out_map, in_map, (((1,), (1,)), ((), ())), preferred_element_type=F32
            ) * triangle
            parts = []
            for pair in range(4):
                mixes = []
                for h in (2 * pair, 2 * pair + 1):
                    gap = jnp.minimum(cumulated[:, h : h + 1] - turned[h : h + 1, :], 0.0)
                    mixes.append((affinity * jnp.exp(gap) * size_turned[h : h + 1, :]).astype(BF16))
                x = xs[strand, rows, 128 * pair : 128 * pair + 128]
                zero = jnp.zeros_like(x)
                tall = jnp.concatenate([jnp.where(left, x, zero), jnp.where(left, zero, x)], axis=0)
                parts.append(jnp.dot(jnp.concatenate(mixes, axis=1), tall, preferred_element_type=F32))
            within = jnp.concatenate(parts, axis=1)
            grown = exact_dot(jnp.exp(cumulated), expand)
            entering = jnp.dot(out_map, starts[strand, g], preferred_element_type=F32) * grown
            local[strand, rows, :] = (within + entering) * gate
            earlier = exact_dot(jnp.broadcast_to(jnp.exp(before), (8, 128)), expand)[0:1]
            carry[strand, rows, :] = grown * earlier * gate
            return before + cumulated[GROUP - 1 :, :]

        lax.fori_loop(0, SPAN // GROUP, one_group, jnp.zeros((1, 128), F32))
        return 0

    lax.fori_loop(0, 2, one_strand, 0)


def finish_kernel(*refs):
    came, refs = refs[:7], refs[7:]
    units, refs = refs[:8], refs[8:]
    prm, maps, local, carry, mine, other, weight, states, entering, wsem, ssem = refs
    z, yl, c, _, _, t = place()
    copies = [pltpu.make_async_copy(came[n], states.at[n], ssem.at[n]) for n in range(7)]
    for n, (unit, f) in enumerate(zip(units, weight_rows())):
        for half in range(2):
            copies.append(
                pltpu.make_async_copy(
                    unit.at[pl.ds(128 + 64 * half, 64)],
                    weight.at[half, pl.ds(pl.multiple_of(64 * f, 64), 64)],
                    wsem.at[2 * n + half],
                )
            )
    fetch(copies)

    def gather(strand, count, slot):
        def one(k, held):
            total, gone = held
            at = slot(k)
            total = total + jnp.exp(gone) * states[at, :STATE, :].astype(F32)
            tail = states[at, STATE:, :].astype(F32)
            return total, gone + tail[0:1] + tail[1:2]

        total, _ = lax.fori_loop(0, count, one, (jnp.zeros((STATE, OWN), F32), jnp.zeros((1, OWN), F32)))
        entering[strand] = total.astype(BF16)

    gather(0, z, lambda k: k)
    gather(1, Z - 1 - z, lambda k: 6 - k)
    gain = prm[5:6, :OWN]
    top = jnp.ones((8, OWN), F32)

    def one_strand(strand, _):
        def one_block(b, _):
            at = pl.multiple_of(ROWS * b, ROWS)
            rows = pl.ds(at, ROWS)
            held = jnp.dot(maps[strand, rows, STATE:], entering[strand], preferred_element_type=F32)
            gated = local[strand, rows, :] + held * carry[strand, rows, :]
            squares = lax.dot_general(
                top, gated * gated, (((1,), (1,)), ((), ())), precision=EXACT, preferred_element_type=F32
            )
            normed = (gated * gain).astype(BF16)
            place_of = jnp.where(strand == 0, b, 3 - b)
            row, core = place_of // 2, lax.rem(place_of, 2)
            row = jnp.where(row == yl, 1, 0)
            hi, lo = hi_lo(squares[0:1])
            line = iota2((8, ROWS), 0)
            tail = jnp.where(line == 0, hi, jnp.where(line == 1, lo, 0.0))

            def put(ref):
                lines = pl.ds(pl.multiple_of(ROWS * strand, ROWS), ROWS)
                for half in range(2):
                    ref[row, lines, 512 * half : 512 * half + 512] = jnp.dot(
                        normed, weight[half], preferred_element_type=F32
                    ).astype(BF16)
                lanes = pl.ds(pl.multiple_of(ROWS * strand, ROWS), ROWS)
                ref[row, 2 * ROWS :, lanes] = jnp.concatenate([tail, jnp.zeros_like(tail)], axis=0).astype(BF16)

            @pl.when(core == c)
            def _():
                put(mine)

            @pl.when(core != c)
            def _():
                put(other)

            return 0

        return lax.fori_loop(0, SPAN // ROWS, one_block, 0)

    for n in range(2):
        mine[n, 2 * ROWS :, 2 * ROWS :] = jnp.zeros((HALO, D - 2 * ROWS), BF16)
        other[n, 2 * ROWS :, 2 * ROWS :] = jnp.zeros((HALO, D - 2 * ROWS), BF16)
    lax.fori_loop(0, 2, one_strand, 0)


def pair_sum(mine, came, out):
    main = mine[0, : 2 * ROWS, :].astype(F32) + came[0, : 2 * ROWS, :].astype(F32)
    out[: 2 * ROWS, :] = main.astype(BF16)
    tail = mine[0, 2 * ROWS :, :].astype(F32) + came[0, 2 * ROWS :, :].astype(F32)
    hi, lo = hi_lo(tail[0:1] + tail[1:2])
    line = iota2((HALO, D), 0)
    out[2 * ROWS :, :] = jnp.where(line == 0, hi, jnp.where(line == 1, lo, 0.0)).astype(BF16)


def last_kernel(mine, came, far, out):
    def tail(ref):
        rows = ref[2 * ROWS :, :].astype(F32)
        return rows[0:1] + rows[1:2]

    squares = tail(mine.at[1]) + tail(came.at[1]) + tail(far)
    diagonal = iota2((ROWS, ROWS), 0) == iota2((ROWS, ROWS), 1)
    for strand in range(2):
        rows = slice(ROWS * strand, ROWS * strand + ROWS)
        mean = jnp.sum(jnp.where(diagonal, squares[:, rows], 0.0), axis=1, keepdims=True) * (1.0 / E)
        main = mine[1, rows, :].astype(F32) + came[1, rows, :].astype(F32) + far[rows, :].astype(F32)
        block = (main * lax.rsqrt(mean + 1e-05)).astype(BF16)
        if strand:
            block = flipped(block)
        out[:, D * strand : D * strand + D] = block


def shape(*dims, dtype=BF16):
    return jax.ShapeDtypeStruct(dims, dtype)


def gathered(own, other):
    far = move(other, lambda z, yl, c, yh, x: dict(yl=1 - yl, yh=1 - yh))
    units = []
    for base in (own, far):
        units.append(base)
        for k in (1, 2, 3):
            units.append(move(base, lambda z, yl, c, yh, x, k=k: dict(x=(x + k) % 4)))
    return units


def swap_core(value):
    return move(value, lambda z, yl, c, yh, x: dict(c=1 - c))


def swap_y(value):
    return move(value, lambda z, yl, c, yh, x: dict(yl=1 - yl))


def halo_step(same):
    def to(z, yl, c, yh, x):
        t = 2 * yl + c
        if t == 3 and z < Z - 1:
            return dict(z=z + 1, yl=1 if same else 0)
        if t == 0 and z > 0:
            return dict(z=z - 1, yl=0 if same else 1)
        return None

    return to


def body(hidden, tokens, base_bias, in_weight, conv_weight, conv_bias, dt_bias, decay_rate, norm_gain, out_weight):
    ua, ua_other, ub, ub_other, prm = pl.pallas_call(
        pack_weights,
        out_shape=[
            shape(128, WA),
            shape(128, WA),
            shape(256, OWN),
            shape(256, OWN),
            shape(8, WA, dtype=F32),
        ],
        in_specs=[VMEM] * 7,
        out_specs=[VMEM] * 5,
        scratch_shapes=[pltpu.VMEM((8, E), F32)],
        name="pack_weights",
        **params(40),
    )(
        in_weight,
        out_weight,
        conv_weight,
        conv_bias[None],
        dt_bias[None],
        decay_rate[None],
        norm_gain[None],
    )
    act, halo = pl.pallas_call(
        prepare_inputs,
        out_shape=[shape(2 * ROWS, D), shape(HALO, D)],
        in_specs=[VMEM] * 3,
        out_specs=[VMEM] * 2,
        name="prepare_inputs",
        **params(40),
    )(hidden[0], tokens, jnp.pad(base_bias, ((0, 3), (0, 0))))
    wa = gathered(ua, ua_other)
    act_y = swap_y(act)
    halo_a = move(halo, halo_step(True))
    halo_b = move(halo, halo_step(False))
    act_c = swap_core(act)
    halo_c = swap_core(halo_a + halo_b)
    act_yc = swap_core(act_y)
    wb = gathered(ub, ub_other)
    blocks = (act, act_y, act_c, act_yc)
    xs, maps, step, starts, *sends = pl.pallas_call(
        scan_kernel,
        out_shape=[
            shape(2, SPAN, OWN),
            shape(2, SPAN, 2 * STATE),
            shape(2, SPAN, 128, dtype=F32),
            shape(2, SPAN // GROUP, STATE, OWN),
        ]
        + [shape(STATE + HALO, OWN)] * 7,
        in_specs=[ANY] * 15 + [VMEM],
        out_specs=[VMEM] * 4 + [ANY] * 7,
        scratch_shapes=[
            pltpu.VMEM((2, PAD, D), BF16),
            pltpu.VMEM((3, HALO, D), BF16),
            pltpu.VMEM((D, WA), BF16),
            pltpu.VMEM((PAD, WA), F32),
            pltpu.VMEM((2, STATE + HALO, OWN), BF16),
            pltpu.SemaphoreType.DMA((8,)),
            pltpu.SemaphoreType.DMA((3,)),
            pltpu.SemaphoreType.DMA((8,)),
            pltpu.SemaphoreType.DMA((7,)),
        ],
        name="scan_kernel",
        **params(56, flops=2 * 1056 * D * WA, bytes_accessed=8 << 20),
    )(*blocks, halo_a, halo_b, halo_c, *wa, prm)
    came = [
        move(sends[k - 1], lambda z, yl, c, yh, x, k=k: dict(z=(z + k) % Z)) for k in range(1, Z)
    ]
    local, carry = pl.pallas_call(
        local_kernel,
        out_shape=[shape(2, SPAN, OWN, dtype=F32)] * 2,
        in_specs=[ANY] * 12 + [VMEM] * 5,
        out_specs=[VMEM] * 2,
        scratch_shapes=[
            pltpu.VMEM((2, PAD, D), BF16),
            pltpu.VMEM((D, OWN), BF16),
            pltpu.SemaphoreType.DMA((8,)),
            pltpu.SemaphoreType.DMA((8,)),
        ],
        name="local_kernel",
        **params(56, flops=4 * 1024 * D * OWN, bytes_accessed=16 << 20),
    )(*blocks, *wb, prm, xs, maps, step, starts)
    mine, other = pl.pallas_call(
        finish_kernel,
        out_shape=[shape(2, 2 * ROWS + HALO, D)] * 2,
        in_specs=[ANY] * 15 + [VMEM] * 4,
        out_specs=[VMEM] * 2,
        scratch_shapes=[
            pltpu.VMEM((2, OWN, 512), BF16),
            pltpu.VMEM((7, STATE + HALO, OWN), BF16),
            pltpu.VMEM((2, STATE, OWN), BF16),
            pltpu.SemaphoreType.DMA((16,)),
            pltpu.SemaphoreType.DMA((7,)),
        ],
        name="finish_kernel",
        **params(56, flops=2 * 1024 * D * OWN, bytes_accessed=8 << 20),
    )(*came, *wb, prm, maps, local, carry)
    core_sum = swap_core(other)
    part = pl.pallas_call(
        pair_sum,
        out_shape=shape(2 * ROWS + HALO, D),
        in_specs=[VMEM] * 2,
        out_specs=VMEM,
        name="pair_sum",
        **params(40),
    )(mine, core_sum)
    far = swap_y(part)
    out = pl.pallas_call(
        last_kernel,
        out_shape=shape(ROWS, 2 * D),
        in_specs=[VMEM] * 3,
        out_specs=VMEM,
        name="last_kernel",
        **params(40),
    )(mine, core_sum, far)
    return out[None]


def solution(mesh):
    placed = (
        P("fsdp", "seq", None),
        P("fsdp", "seq"),
        P(),
        P("fsdp", None),
        P(),
        P(),
        P(),
        P(),
        P(),
        P("fsdp", None),
    )
    return jax.shard_map(
        body, mesh=mesh, in_specs=placed, out_specs=P("fsdp", "seq", None), check_vma=False
    )
```

```python
import jax
import jax.numpy as jnp
from jax import lax
from jax.experimental import pallas as pl
from jax.experimental.pallas import tpu as pltpu
from jax.sharding import PartitionSpec as P

D = 1024
HEADS = 32
HEADDIM = 64
STATE = 128
CONV = 4
GROUP = 128
E = 2048
WIDE = 4384
ROWS = 128
SPAN = 512
GROUPS = SPAN // GROUP
OWN = 512
MINE = 8
HALO = 16
PAD = HALO + SPAN
CONVED = OWN + 2 * STATE
WA = CONVED + 128
UNIT = 176
Z = 8
PAYLOAD = 4 * ROWS + HALO + 4 * 48

F32 = jnp.float32
BF16 = jnp.bfloat16
EXACT = lax.Precision.HIGHEST
ANY = pl.BlockSpec(memory_space=pl.ANY)
VMEM = pl.BlockSpec(memory_space=pltpu.VMEM)


def place():
    s, f = lax.axis_index("seq"), lax.axis_index("fsdp")
    t = lax.rem(s, 4)
    return s // 4, t // 2, lax.rem(t, 2), f // 4, lax.rem(f, 4), t


def move(value, to):
    pairs = []
    for s in range(32):
        for f in range(8):
            here = dict(z=s // 4, yl=(s // 2) % 2, c=s % 2, yh=f // 4, x=f % 4)
            change = to(**here)
            if change is None:
                continue
            there = {**here, **change}
            target = (there["z"] * 4 + there["yl"] * 2 + there["c"]) * 8 + there["yh"] * 4 + there["x"]
            pairs.append((s * 8 + f, target))
    return lax.ppermute(value, ("seq", "fsdp"), pairs)


def shape(*dims, dtype=BF16):
    return jax.ShapeDtypeStruct(dims, dtype)


def call(kernel, name, outs, ins, operands, scratch=(), mb=48, flops=0, bytes_accessed=0, out_specs=None):
    return pl.pallas_call(
        kernel,
        out_shape=outs,
        in_specs=ins,
        out_specs=jax.tree.map(lambda _: VMEM, outs) if out_specs is None else out_specs,
        scratch_shapes=scratch,
        name=name,
        compiler_params=pltpu.CompilerParams(vmem_limit_bytes=mb << 20),
        cost_estimate=pl.CostEstimate(flops=flops, bytes_accessed=bytes_accessed, transcendentals=0),
    )(*operands)


def after(value, *others):
    def kernel(*refs):
        refs[-1][...] = refs[0][...]

    return call(
        kernel,
        "after",
        shape(*value.shape, dtype=value.dtype),
        [VMEM] * (1 + len(others)),
        (value, *others),
    )


def iota2(dims, dim):
    return lax.broadcasted_iota(jnp.int32, dims, dim)


def ones_at(where):
    return jnp.where(where, 1.0, 0.0)


def anti_identity():
    return ones_at(iota2((128, 128), 0) + iota2((128, 128), 1) == 127).astype(BF16)


def flipped(block):
    anti = anti_identity()
    rows = jnp.dot(anti, block, preferred_element_type=F32).astype(BF16)
    parts = [
        jnp.dot(rows[:, 128 * j : 128 * j + 128], anti, preferred_element_type=F32).astype(BF16)
        for j in range(D // 128)
    ]
    return jnp.concatenate(parts[::-1], axis=1)


def head_pick():
    _, yl, c, _, _, t = place()
    t_other = (1 - yl) * 2 + c
    row, col = iota2((512, 256), 0), iota2((512, 256), 1)
    inner = lax.rem(col, 128)
    head = jnp.where(col < 128, t, t_other)
    return ones_at(row == 256 * (inner // 64) + 64 * head + lax.rem(inner, 64))


def tiles():
    for lane in range(3):
        for group in range(4):
            n = lane * 4 + group
            yield lane, group, slice(ROWS + 16 * (n % 3), ROWS + 16 * (n % 3) + 16), slice(128 * (n // 3), 128 * (n // 3) + 128)


def pack_input_weight(iw, ua, ua_other, held, sem):
    _, yl, c, _, _, _ = place()
    copy = pltpu.make_async_copy(iw.at[:, E:], held, sem)
    copy.start()
    pick = head_pick().astype(BF16)
    lane, out = iota2((HEADS, 256), 0), iota2((HEADS, 256), 1)
    inner = lax.rem(out, 128)
    both_cores = 4 * lax.rem(inner, MINE) + 2 * jnp.where(out < 128, yl, 1 - yl) + inner // MINE
    step_pick = ones_at((lane == both_cores) & (inner < 2 * MINE)).astype(BF16)
    copy.wait()
    for j in range(4):
        got = jnp.dot(held[:, 512 * j : 512 * j + 512], pick, preferred_element_type=F32).astype(BF16)
        ua[:ROWS, 128 * j : 128 * j + 128] = got[:, :128]
        ua_other[:ROWS, 128 * j : 128 * j + 128] = got[:, 128:]
    rows = pl.ds(pl.multiple_of(64 * c, 64), 64)
    steps = jnp.dot(held[rows, E + 2 * STATE :], step_pick, preferred_element_type=F32).astype(BF16)
    for lane, group, line, cols in tiles():
        part = slice(16 * group, 16 * group + 16)
        if lane < 2:
            block = held[rows, E + 128 * lane : E + 128 * lane + 128][part]
            ua[line, cols] = block
            ua_other[line, cols] = block
        else:
            ua[line, cols] = steps[part, :128]
            ua_other[line, cols] = steps[part, 128:]


def pack_late_weights(iw, ow, cw, cb, dtb, rate, gain, ub, ub_other, prm, heads, stack):
    _, yl, c, _, _, t = place()
    t_other = (1 - yl) * 2 + c
    pick = head_pick()
    pick_bf = pick.astype(BF16)
    for j in range(4):
        got = jnp.dot(iw[:, 512 * j : 512 * j + 512], pick_bf, preferred_element_type=F32).astype(BF16)
        ub[:ROWS, 128 * j : 128 * j + 128] = got[:, :128]
        ub_other[:ROWS, 128 * j : 128 * j + 128] = got[:, 128:]
    for ref, which in ((ub, t), (ub_other, t_other)):
        rows = ow[pl.ds(pl.multiple_of(64 * which, 64), 64), :]
        ref[128:192, :] = rows[:, :512]
        ref[192:256, :] = rows[:, 512:]
    stack[...] = jnp.zeros_like(stack)
    stack[0:4, :] = cw[:, :E]
    stack[4:5, :] = cb[:, :E]
    stack[5:6, :] = gain[...]
    prm[...] = jnp.zeros_like(prm)
    for j in range(4):
        prm[:, 128 * j : 128 * j + 128] = jnp.dot(
            stack[:, 512 * j : 512 * j + 512], pick[:, :128], precision=EXACT, preferred_element_type=F32
        )
    prm[0:4, OWN:] = cw[:, E:]
    prm[4:5, OWN:] = cb[:, E:]
    chosen = iota2((MINE, HEADS), 1) == 4 * iota2((MINE, HEADS), 0) + t
    for n, ref in enumerate((dtb, rate)):
        column = jnp.sum(jnp.where(chosen, ref[...], 0.0), axis=1, keepdims=True)
        heads[n] = jnp.broadcast_to(column, (MINE, 128))


def prepare_inputs(hidden, tokens, base_bias, act, halo):
    _, _, c, _, _, _ = place()
    ids = tokens[...]
    letter = iota2((5, ROWS), 0)
    paired = jnp.where(ids == 4, 4, 3 - ids)
    for strand, chosen in ((0, ids), (1, paired)):
        onehot = ones_at(letter == chosen).astype(BF16)
        bias = lax.dot_general(
            onehot, base_bias[:, D * strand : D * strand + D], (((0,), (0,)), ((), ())), preferred_element_type=F32
        )
        block = (hidden[:, D * strand : D * strand + D].astype(F32) + bias).astype(BF16)
        if strand:
            block = flipped(block)
        act[ROWS * strand : ROWS * strand + ROWS, :] = block
    halo[...] = jnp.where(c == 1, act[ROWS - HALO : ROWS, :], act[2 * ROWS - HALO :, :])


def pack_core(*refs):
    act, act_y, halo_a, halo_b = refs[:4]
    units, out = refs[4:12], refs[12]
    out[: 2 * ROWS, :] = act[...]
    out[2 * ROWS : 4 * ROWS, :] = act_y[...]
    out[4 * ROWS : 4 * ROWS + HALO, :] = halo_a[...] + halo_b[...]
    for n, unit in enumerate(units):
        line = 4 * ROWS + HALO + 48 * (n % 4)
        out[line : line + 48, 512 * (n // 4) : 512 * (n // 4) + 512] = unit[ROWS:, :]


def weight_rows():
    _, _, _, yh, x, _ = place()
    return [which * 4 + lax.rem(x - k + 4, 4) for which in (yh, 1 - yh) for k in range(4)]


def place_act(act, blocks):
    _, _, _, _, _, t = place()
    for (ref, first), other in zip(blocks, (0, 2, 1, 3)):
        at = t ^ other
        for strand, row in ((0, at), (1, 3 - at)):
            act[strand, pl.ds(pl.multiple_of(HALO + ROWS * row, 16), ROWS), :] = ref[
                first + ROWS * strand : first + ROWS * strand + ROWS, :
            ]


def spread_heads(count):
    return ones_at(lax.rem(iota2((MINE * count, OWN), 0), MINE) == iota2((MINE * count, OWN), 1) // HEADDIM)


def hi_lo(v):
    hi = v.astype(BF16).astype(F32)
    return hi, v - hi


def spread_columns(rows):
    both = jnp.concatenate(hi_lo(rows), axis=0).astype(BF16)
    return lax.dot_general(
        both, spread_heads(2).astype(BF16), (((0,), (0,)), ((), ())), preferred_element_type=F32
    )


def spread_row(column):
    return jnp.sum(spread_heads(1) * column, axis=0, keepdims=True)


def running_sum(rows):
    count = rows.shape[0]
    hi, rest = hi_lo(rows)
    mid, low = hi_lo(rest)
    upper = ones_at(iota2((GROUP, GROUP), 0) <= iota2((GROUP, GROUP), 1)).astype(BF16)
    pieces = jnp.concatenate([hi, mid, low], axis=0).astype(BF16)
    sums = jnp.dot(pieces, upper, preferred_element_type=F32)
    return sums[:count] + sums[count : 2 * count] + sums[2 * count :]


def scan_kernel(*refs):
    act_own, act_y, halo_a, halo_b, swapped = refs[:5]
    units, refs = refs[5:13], refs[13:]
    prm, heads, refs = refs[0], refs[1], refs[2:]
    xs, maps, sizes, sums, starts, *sends = refs[:12]
    act, weight, proj, ends = refs[12:]
    z, _, c, _, _, _ = place()
    for n, (unit, f) in enumerate(zip(units, weight_rows())):
        weight[pl.ds(pl.multiple_of(ROWS * f, ROWS), ROWS), :OWN] = unit[:ROWS, :]
        for lane, group, line, cols in tiles():
            left = OWN + 128 * lane
            row = pl.multiple_of(ROWS * f + 64 * c + 16 * group, 16)
            weight[pl.ds(row, 16), left : left + 128] = unit[line, cols]
            row = pl.multiple_of(ROWS * f + 64 * (1 - c) + 16 * group, 16)
            first = 4 * ROWS + HALO + 48 * (n % 4) + line.start - ROWS
            side = 512 * (n // 4) + cols.start
            weight[pl.ds(row, 16), left : left + 128] = swapped[first : first + 16, side : side + 128]
    place_act(act, ((act_own, 0), (act_y, 0), (swapped, 0), (swapped, 2 * ROWS)))
    near = halo_a[...] + halo_b[...]
    far = swapped[4 * ROWS : 4 * ROWS + HALO, :]
    act[0, :HALO, :] = jnp.where(c == 1, near, far)
    act[1, :HALO, :] = jnp.where(c == 1, far, near)

    def one_strand(strand, _):
        proj[...] = jnp.dot(act[strand], weight[...], preferred_element_type=F32).astype(BF16).astype(F32)
        turned = []
        for g in range(GROUPS):
            steps = proj[HALO + GROUP * g : HALO + GROUP * g + GROUP, CONVED:].T
            turned.append(jnp.where(c == 0, steps[:MINE], steps[MINE : 2 * MINE]))
        raw = jnp.concatenate(turned, axis=0) + jnp.concatenate([heads[0]] * GROUPS, axis=0)
        size = jnp.maximum(raw, 0.0) + jnp.log1p(jnp.exp(-jnp.abs(raw)))
        decay = -size * jnp.concatenate([heads[1]] * GROUPS, axis=0)
        cumulated = running_sum(decay)
        sizes[strand] = size
        sums[strand] = cumulated
        state = jnp.zeros((STATE, OWN), F32)
        total = jnp.zeros((MINE, 1), F32)
        for g in range(GROUPS):
            rows = slice(GROUP * g, GROUP * g + GROUP)
            for j in range(6):
                cols = slice(128 * j, 128 * j + 128)
                first = HALO - 3 + GROUP * g
                acc = prm[4:5, cols] + prm[0:1, cols] * proj[first : first + GROUP, cols]
                for k in range(1, CONV):
                    acc = acc + prm[k : k + 1, cols] * proj[first + k : first + k + GROUP, cols]
                half = 0.5 * acc
                done = (half + half * jnp.tanh(half)).astype(BF16)
                if j < 4:
                    xs[strand, rows, cols] = done
                else:
                    maps[strand, rows, 128 * (j - 4) : 128 * (j - 4) + 128] = done
            part = slice(MINE * g, MINE * g + MINE)
            last = cumulated[part, GROUP - 1 :]
            total = total + last
            remaining = spread_columns(jnp.exp(last - cumulated[part]) * size[part])
            weighted = (xs[strand, rows, :].astype(F32) * remaining).astype(BF16)
            starts[strand, g] = state.astype(BF16)
            added = lax.dot_general(
                maps[strand, rows, :STATE], weighted, (((0,), (0,)), ((), ())), preferred_element_type=F32
            )
            state = state * spread_row(jnp.exp(last)) + added
        ends[strand, :STATE, :] = state.astype(BF16)
        hi, lo = hi_lo(spread_row(total))
        line = iota2((HALO, OWN), 0)
        ends[strand, STATE:, :] = jnp.where(line == 0, hi, jnp.where(line == 1, lo, 0.0)).astype(BF16)
        return 0

    lax.fori_loop(0, 2, one_strand, 0)
    for k in range(1, Z):
        strand = jnp.where(z + k < Z, 0, 1)
        sends[k - 1][...] = ends[strand]


def local_kernel(*refs):
    xs, maps, sizes, sums, starts, local, carry = refs
    causal = ones_at(iota2((GROUP, GROUP), 0) >= iota2((GROUP, GROUP), 1))
    left = iota2((GROUP, 128), 1) < HEADDIM

    def one_strand(strand, _):
        def one_group(g, before):
            rows = pl.ds(pl.multiple_of(GROUP * g, GROUP), GROUP)
            part = pl.ds(pl.multiple_of(MINE * g, MINE), MINE)
            size = sizes[strand, part, :]
            cumulated = sums[strand, part, :]
            columns = jnp.concatenate([cumulated, jnp.zeros((GROUP - MINE, GROUP), F32)], axis=0).T
            in_map = maps[strand, rows, :STATE]
            out_map = maps[strand, rows, STATE:]
            affinity = lax.dot_general(
                out_map, in_map, (((1,), (1,)), ((), ())), preferred_element_type=F32
            ) * causal
            parts = []
            for pair in range(4):
                mixes = []
                for h in (2 * pair, 2 * pair + 1):
                    gap = jnp.minimum(columns[:, h : h + 1] - cumulated[h : h + 1, :], 0.0)
                    mixes.append((affinity * jnp.exp(gap) * size[h : h + 1, :]).astype(BF16))
                x = xs[strand, rows, 128 * pair : 128 * pair + 128]
                zero = jnp.zeros_like(x)
                tall = jnp.concatenate([jnp.where(left, x, zero), jnp.where(left, zero, x)], axis=0)
                parts.append(jnp.dot(jnp.concatenate(mixes, axis=1), tall, preferred_element_type=F32))
            within = jnp.concatenate(parts, axis=1)
            grown = spread_columns(jnp.exp(cumulated))
            local[strand, rows, :] = within + jnp.dot(out_map, starts[strand, g], preferred_element_type=F32) * grown
            carry[strand, rows, :] = grown * spread_row(jnp.exp(before))
            return before + cumulated[:, GROUP - 1 :]

        lax.fori_loop(0, GROUPS, one_group, jnp.zeros((MINE, 1), F32))
        return 0

    lax.fori_loop(0, 2, one_strand, 0)


def gate_kernel(*refs):
    act_own, act_y, swapped = refs[:3]
    units, refs = refs[3:11], refs[11:]
    local, carry, gated, gated_carry, out_weight, act, weight = refs
    for unit, f in zip(units, weight_rows()):
        weight[pl.ds(pl.multiple_of(ROWS * f, ROWS), ROWS), :] = unit[:ROWS, :]
        for half in range(2):
            rows = unit[ROWS + 64 * half : ROWS + 64 * half + 64, :]
            out_weight[half, pl.ds(pl.multiple_of(64 * f, 64), 64), :] = rows
    place_act(act, ((act_own, 0), (act_y, 0), (swapped, 0), (swapped, 2 * ROWS)))

    def one_strand(strand, _):
        for g in range(2):
            rows = slice(256 * g, 256 * g + 256)
            gate = jnp.dot(
                act[strand, HALO + 256 * g : HALO + 256 * g + 256, :], weight[...], preferred_element_type=F32
            )
            half = 0.5 * gate.astype(BF16).astype(F32)
            gate = half + half * jnp.tanh(half)
            gated[strand, rows, :] = local[strand, rows, :] * gate
            gated_carry[strand, rows, :] = carry[strand, rows, :] * gate
        return 0

    lax.fori_loop(0, 2, one_strand, 0)


def half_rows(own):
    _, yl, _, _, _, _ = place()
    y = yl if own else 1 - yl
    return 256 * y, 256 * (1 - y)


def project_half(own, weight, entering, prm, maps, local, carry, keep, give, normed):
    _, _, c, _, _, _ = place()
    gain = prm[5:6, :OWN]
    tails = []
    for strand, first in enumerate(half_rows(own)):
        for b in range(2):
            rows = pl.ds(pl.multiple_of(first + ROWS * b, ROWS), ROWS)
            held = jnp.dot(maps[strand, rows, STATE:], entering[strand], preferred_element_type=F32)
            gated = local[strand, rows, :] + held * carry[strand, rows, :]
            squared = gated * gated
            folded = (squared[:, :128] + squared[:, 128:256]) + (squared[:, 256:384] + squared[:, 384:])
            tails.append(jnp.sum(folded.T, axis=0, keepdims=True))
            normed[2 * strand + b] = (gated * gain).astype(BF16)
    line = iota2((HALO, ROWS), 0)
    for ref, core in ((keep, c), (give, 1 - c)):
        for strand in range(2):
            b = core if strand == 0 else 1 - core
            for half in range(2):
                ref[ROWS * strand : ROWS * strand + ROWS, 512 * half : 512 * half + 512] = jnp.dot(
                    normed[2 * strand + b], weight[half], preferred_element_type=F32
                ).astype(BF16)
            hi, lo = hi_lo(jnp.where(b == 0, tails[2 * strand], tails[2 * strand + 1]))
            tail = jnp.where(line == 0, hi, jnp.where(line == 1, lo, 0.0))
            ref[2 * ROWS :, ROWS * strand : ROWS * strand + ROWS] = tail.astype(BF16)
        ref[2 * ROWS :, 2 * ROWS :] = jnp.zeros((HALO, D - 2 * ROWS), BF16)


def first_half(*refs):
    came, refs = refs[:7], refs[7:]
    weight, prm, maps, local, carry, entering, keep, give, normed, total = refs
    z, _, _, _, _, _ = place()
    total[...] = jnp.zeros_like(total)
    for strand in range(2):
        gone = jnp.zeros((1, OWN), F32)
        for k in range(Z - 1):
            ref = came[k] if strand == 0 else came[6 - k]
            here = k < z if strand == 0 else k < Z - 1 - z
            factor = jnp.exp(gone)

            @pl.when(here)
            def _(ref=ref, factor=factor):
                total[strand] += factor * ref[:STATE, :].astype(F32)

            tail = ref[STATE:, :].astype(F32)
            gone = gone + jnp.where(here, tail[0:1] + tail[1:2], 0.0)
        entering[strand] = total[strand].astype(BF16)
    project_half(False, weight, entering, prm, maps, local, carry, keep, give, normed)


def second_half(part, weight, entering, prm, maps, local, carry, keep, give, normed):
    project_half(True, weight, entering, prm, maps, local, carry, keep, give, normed)


def pair_sum(mine, came, out):
    main = mine[: 2 * ROWS, :].astype(F32) + came[: 2 * ROWS, :].astype(F32)
    out[: 2 * ROWS, :] = main.astype(BF16)
    tail = mine[2 * ROWS :, :].astype(F32) + came[2 * ROWS :, :].astype(F32)
    hi, lo = hi_lo(tail[0:1] + tail[1:2])
    line = iota2((HALO, D), 0)
    out[2 * ROWS :, :] = jnp.where(line == 0, hi, jnp.where(line == 1, lo, 0.0)).astype(BF16)


def last_kernel(mine, came, far, out):
    def tail(ref):
        rows = ref[2 * ROWS :, :].astype(F32)
        return rows[0:1] + rows[1:2]

    squares = tail(mine) + tail(came) + tail(far)
    diagonal = iota2((ROWS, ROWS), 0) == iota2((ROWS, ROWS), 1)
    for strand in range(2):
        rows = slice(ROWS * strand, ROWS * strand + ROWS)
        mean = jnp.sum(jnp.where(diagonal, squares[:, rows], 0.0), axis=1, keepdims=True) * (1.0 / E)
        main = mine[rows, :].astype(F32) + came[rows, :].astype(F32) + far[rows, :].astype(F32)
        block = (main * lax.rsqrt(mean + 1e-05)).astype(BF16)
        if strand:
            block = flipped(block)
        out[:, D * strand : D * strand + D] = block


def gathered(own, other):
    far = swap_diagonal(other)
    return [own] + [along_x(own, k) for k in (1, 2, 3)] + [far] + [along_x(far, k) for k in (1, 2, 3)]


def swap_core(value):
    return move(value, lambda z, yl, c, yh, x: dict(c=1 - c))


def swap_y(value):
    return move(value, lambda z, yl, c, yh, x: dict(yl=1 - yl))


def swap_diagonal(value, k=0):
    return move(value, lambda z, yl, c, yh, x: dict(yl=1 - yl, yh=1 - yh, x=(x + k) % 4))


def along_x(value, k):
    return move(value, lambda z, yl, c, yh, x: dict(x=(x + k) % 4))


def along_z(value, k):
    return move(value, lambda z, yl, c, yh, x: dict(z=(z + k) % Z))


def halo_step(same):
    def to(z, yl, c, yh, x):
        t = 2 * yl + c
        if t == 3 and z < Z - 1:
            return dict(z=z + 1, yl=1 if same else 0)
        if t == 0 and z > 0:
            return dict(z=z - 1, yl=0 if same else 1)
        return None

    return to


def body(hidden, tokens, base_bias, in_weight, conv_weight, conv_bias, dt_bias, decay_rate, norm_gain, out_weight):
    ua, ua_other = call(
        pack_input_weight,
        "pack_input_weight",
        [shape(UNIT, OWN)] * 2,
        [ANY],
        (in_weight,),
        scratch=[pltpu.VMEM((ROWS, WIDE - E), BF16), pltpu.SemaphoreType.DMA(())],
    )
    act, halo = call(
        prepare_inputs,
        "prepare_inputs",
        [shape(2 * ROWS, D), shape(HALO, D)],
        [VMEM] * 3,
        (hidden[0], tokens, base_bias),
    )
    act_y = swap_y(act)
    units = gathered(ua, ua_other)
    halo_a = move(halo, halo_step(True))
    halo_b = move(halo, halo_step(False))
    swapped = swap_core(
        call(
            pack_core, "pack_core", shape(PAYLOAD, D), [VMEM] * 12, (act, act_y, halo_a, halo_b, *units)
        )
    )
    ub, ub_other, prm, heads = call(
        pack_late_weights,
        "pack_late_weights",
        [shape(256, OWN), shape(256, OWN), shape(8, CONVED, dtype=F32), shape(2, MINE, 128, dtype=F32)],
        [VMEM] * 7,
        (in_weight, out_weight, conv_weight, conv_bias[None], dt_bias[None], decay_rate[None], norm_gain[None]),
        scratch=[pltpu.VMEM((8, E), F32)],
    )
    late = gathered(ub, ub_other)
    xs, maps, sizes, sums, starts, *sends = call(
        scan_kernel,
        "scan_kernel",
        [
            shape(2, SPAN, OWN),
            shape(2, SPAN, 2 * STATE),
            shape(2, MINE * GROUPS, GROUP, dtype=F32),
            shape(2, MINE * GROUPS, GROUP, dtype=F32),
            shape(2, GROUPS, STATE, OWN),
        ]
        + [shape(STATE + HALO, OWN)] * 7,
        [VMEM] * 15,
        (act, act_y, halo_a, halo_b, swapped, *units, prm, heads),
        scratch=[
            pltpu.VMEM((2, PAD, D), BF16),
            pltpu.VMEM((D, WA), BF16),
            pltpu.VMEM((PAD, WA), F32),
            pltpu.VMEM((2, STATE + HALO, OWN), BF16),
        ],
        flops=2 * 1056 * D * WA,
        bytes_accessed=8 << 20,
    )
    came = [along_z(sends[k - 1], k) for k in range(1, Z)]
    local, carry = call(
        local_kernel,
        "local_kernel",
        [shape(2, SPAN, OWN, dtype=F32)] * 2,
        [VMEM] * 5,
        (xs, maps, sizes, sums, starts),
        flops=4 * 1024 * D * OWN,
        bytes_accessed=16 << 20,
    )
    local, carry, weight = call(
        gate_kernel,
        "gate_kernel",
        [shape(2, SPAN, OWN, dtype=F32)] * 2 + [shape(2, OWN, 512)],
        [VMEM] * 13,
        (act, act_y, swapped, *late, local, carry),
        scratch=[pltpu.VMEM((2, PAD, D), BF16), pltpu.VMEM((D, OWN), BF16)],
        flops=2 * 1024 * D * OWN,
        bytes_accessed=8 << 20,
    )
    half_out = [shape(2 * ROWS + HALO, D)] * 2
    half_scratch = [pltpu.VMEM((4, ROWS, OWN), BF16)]
    entering, keep, give = call(
        first_half,
        "first_half",
        [shape(2, STATE, OWN)] + half_out,
        [VMEM] * 12,
        (*came, weight, prm, maps, local, carry),
        scratch=half_scratch + [pltpu.VMEM((2, STATE, OWN), F32)],
        flops=1024 * D * OWN,
        bytes_accessed=4 << 20,
    )
    part = call(pair_sum, "pair_sum", shape(2 * ROWS + HALO, D), [VMEM] * 2, (keep, swap_core(give)))
    far_part = swap_y(part)
    keep, give = call(
        second_half,
        "second_half",
        half_out,
        [VMEM] * 7,
        (part, weight, entering, prm, maps, local, carry),
        scratch=half_scratch,
        flops=32 * 1024 * D * OWN,
        bytes_accessed=4 << 20,
    )
    out = call(last_kernel, "last_kernel", shape(ROWS, 2 * D), [VMEM] * 3, (keep, swap_core(give), far_part))
    return out[None]


def solution(mesh):
    placed = (
        P("fsdp", "seq", None),
        P("fsdp", "seq"),
        P(),
        P("fsdp", None),
        P(),
        P(),
        P(),
        P(),
        P(),
        P("fsdp", None),
    )
    return jax.shard_map(
        body, mesh=mesh, in_specs=placed, out_specs=P("fsdp", "seq", None), check_vma=False
    )
```

```python
import jax
import jax.numpy as jnp
from jax import lax
from jax.experimental import pallas as pl
from jax.experimental.pallas import tpu as pltpu
from jax.sharding import PartitionSpec as P

D = 1024
HEADS = 32
HEADDIM = 64
STATE = 128
CONV = 4
GROUP = 128
E = 2048
WIDE = 4384
ROWS = 128
SPAN = 512
GROUPS = SPAN // GROUP
OWN = 512
MINE = 8
HALO = 16
PAD = HALO + SPAN
CONVED = OWN + 2 * STATE
WA = CONVED + 128
UNIT = OWN + STATE + HEADS
LATE = 2 * HEADDIM
Z = 8
PAYLOAD = 4 * ROWS + HALO + STATE

F32 = jnp.float32
BF16 = jnp.bfloat16
EXACT = lax.Precision.HIGHEST
ANY = pl.BlockSpec(memory_space=pl.ANY)
VMEM = pl.BlockSpec(memory_space=pltpu.VMEM)


def place():
    s, f = lax.axis_index("seq"), lax.axis_index("fsdp")
    t = lax.rem(s, 4)
    return s // 4, t // 2, lax.rem(t, 2), f // 4, lax.rem(f, 4), t


def move(value, to):
    pairs = []
    for s in range(32):
        for f in range(8):
            here = dict(z=s // 4, yl=(s // 2) % 2, c=s % 2, yh=f // 4, x=f % 4)
            change = to(**here)
            if change is None:
                continue
            there = {**here, **change}
            target = (there["z"] * 4 + there["yl"] * 2 + there["c"]) * 8 + there["yh"] * 4 + there["x"]
            pairs.append((s * 8 + f, target))
    return lax.ppermute(value, ("seq", "fsdp"), pairs)


def shape(*dims, dtype=BF16):
    return jax.ShapeDtypeStruct(dims, dtype)


def call(kernel, name, outs, ins, operands, scratch=(), mb=48, flops=0, bytes_accessed=0, out_specs=None):
    return pl.pallas_call(
        kernel,
        out_shape=outs,
        in_specs=ins,
        out_specs=jax.tree.map(lambda _: VMEM, outs) if out_specs is None else out_specs,
        scratch_shapes=scratch,
        name=name,
        compiler_params=pltpu.CompilerParams(vmem_limit_bytes=mb << 20),
        cost_estimate=pl.CostEstimate(flops=flops, bytes_accessed=bytes_accessed, transcendentals=0),
    )(*operands)


def iota2(dims, dim):
    return lax.broadcasted_iota(jnp.int32, dims, dim)


def ones_at(where):
    return jnp.where(where, 1.0, 0.0)


def anti_identity():
    return ones_at(iota2((128, 128), 0) + iota2((128, 128), 1) == 127).astype(BF16)


def flipped(block):
    anti = anti_identity()
    rows = jnp.dot(anti, block, preferred_element_type=F32).astype(BF16)
    parts = [
        jnp.dot(rows[:, 128 * j : 128 * j + 128], anti, preferred_element_type=F32).astype(BF16)
        for j in range(D // 128)
    ]
    return jnp.concatenate(parts[::-1], axis=1)


def head_pick():
    _, _, _, _, _, t = place()
    row, col = iota2((512, 128), 0), iota2((512, 128), 1)
    return ones_at(row == 256 * (col // 64) + 64 * t + lax.rem(col, 64))


def start_kernel(hidden, tokens, base_bias, iw, ow, act, halo, ua, ua_other, ub, ub_other, rows_in, ids_in, bias_in, iw_in, ow_in, sem):
    _, yl, c, _, _, t = place()
    copies = [
        pltpu.make_async_copy(tokens, ids_in, sem.at[0]),
        pltpu.make_async_copy(base_bias, bias_in, sem.at[1]),
        pltpu.make_async_copy(hidden, rows_in, sem.at[2]),
        pltpu.make_async_copy(iw.at[pl.ds(E, WIDE - E)], iw_in.at[pl.ds(E, WIDE - E)], sem.at[3]),
        pltpu.make_async_copy(iw.at[pl.ds(0, E)], iw_in.at[pl.ds(0, E)], sem.at[4]),
        pltpu.make_async_copy(ow, ow_in, sem.at[5]),
    ]
    for copy in copies:
        copy.start()
    for copy in copies[:3]:
        copy.wait()
    ids = ids_in[...]
    letter = iota2((5, ROWS), 0)
    paired = jnp.where(ids == 4, 4, 3 - ids)
    for strand, chosen in ((0, ids), (1, paired)):
        onehot = ones_at(letter == chosen).astype(BF16)
        bias = lax.dot_general(
            onehot, bias_in[:, D * strand : D * strand + D], (((0,), (0,)), ((), ())), preferred_element_type=F32
        )
        block = (rows_in[:, D * strand : D * strand + D].astype(F32) + bias).astype(BF16)
        if strand:
            block = flipped(block)
        act[ROWS * strand : ROWS * strand + ROWS, :] = block
    halo[...] = jnp.where(c == 1, act[ROWS - HALO : ROWS, :], act[2 * ROWS - HALO :, :])
    for copy in copies[3:]:
        copy.wait()
    for early, late, which in ((ua, ub, t), (ua_other, ub_other, (1 - yl) * 2 + c)):
        for j in range(MINE):
            row = pl.multiple_of(256 * j + 64 * which, 64)
            early[64 * j : 64 * j + 64, :] = iw_in[pl.ds(E + row, 64), :]
            late[:HEADDIM, 128 * j : 128 * j + 128] = iw_in[pl.ds(row, 64), :]
        early[OWN : OWN + STATE, :] = iw_in[pl.ds(pl.multiple_of(2 * E + STATE * c, STATE), STATE), :]
        early[OWN + STATE :, :] = iw_in[2 * E + 2 * STATE :, :]
        late[HEADDIM:, :] = ow_in[pl.ds(pl.multiple_of(64 * which, 64), 64), :]


def hold(*refs):
    count = (len(refs) - 1) // 2
    for n in range(count):
        refs[count + 1 + n][...] = refs[n][...]


def pack_params(cw, cb, dtb, rate, gain, prm, heads, stack):
    _, _, _, _, _, t = place()
    pick = head_pick()
    stack[...] = jnp.zeros_like(stack)
    stack[0:4, :] = cw[:, :E]
    stack[4:5, :] = cb[:, :E]
    stack[5:6, :] = gain[...]
    prm[...] = jnp.zeros_like(prm)
    for j in range(4):
        prm[:, 128 * j : 128 * j + 128] = jnp.dot(
            stack[:, 512 * j : 512 * j + 512], pick, precision=EXACT, preferred_element_type=F32
        )
    prm[0:4, OWN:] = cw[:, E:]
    prm[4:5, OWN:] = cb[:, E:]
    chosen = iota2((MINE, HEADS), 1) == 4 * iota2((MINE, HEADS), 0) + t
    for n, ref in enumerate((dtb, rate)):
        column = jnp.sum(jnp.where(chosen, ref[...], 0.0), axis=1, keepdims=True)
        heads[n] = jnp.broadcast_to(column, (MINE, 128))


def pack_core(*refs):
    act, act_y, halo_a, halo_b, ub, ub_far = refs[:6]
    units, out, out_b = refs[6:14], refs[14], refs[15]
    out_b[:LATE, :] = ub[...]
    out_b[LATE:, :] = ub_far[...]
    out[: 2 * ROWS, :] = act[...]
    out[2 * ROWS : 4 * ROWS, :] = act_y[...]
    out[4 * ROWS : 4 * ROWS + HALO, :] = halo_a[...] + halo_b[...]
    for n, unit in enumerate(units):
        out[4 * ROWS + HALO :, 128 * n : 128 * n + 128] = unit[OWN : OWN + STATE, :]


def weight_rows():
    _, _, _, yh, x, _ = place()
    return [which * 4 + lax.rem(x - k + 4, 4) for which in (yh, 1 - yh) for k in range(4)]


def place_act(act, blocks):
    _, _, _, _, _, t = place()
    for (ref, first), other in zip(blocks, (0, 2, 1, 3)):
        at = t ^ other
        for strand, row in ((0, at), (1, 3 - at)):
            act[strand, pl.ds(pl.multiple_of(HALO + ROWS * row, 16), ROWS), :] = ref[
                first + ROWS * strand : first + ROWS * strand + ROWS, :
            ]


def spread_heads(count):
    return ones_at(lax.rem(iota2((MINE * count, OWN), 0), MINE) == iota2((MINE * count, OWN), 1) // HEADDIM)


def hi_lo(v):
    hi = v.astype(BF16).astype(F32)
    return hi, v - hi


def spread_columns(rows):
    both = jnp.concatenate(hi_lo(rows), axis=0).astype(BF16)
    return lax.dot_general(
        both, spread_heads(2).astype(BF16), (((0,), (0,)), ((), ())), preferred_element_type=F32
    )


def spread_row(column):
    return jnp.sum(spread_heads(1) * column, axis=0, keepdims=True)


def running_sum(rows):
    count = rows.shape[0]
    hi, rest = hi_lo(rows)
    mid, low = hi_lo(rest)
    upper = ones_at(iota2((GROUP, GROUP), 0) <= iota2((GROUP, GROUP), 1)).astype(BF16)
    pieces = jnp.concatenate([hi, mid, low], axis=0).astype(BF16)
    sums = jnp.dot(pieces, upper, preferred_element_type=F32)
    return sums[:count] + sums[count : 2 * count] + sums[2 * count :]


def times_turned(a, b):
    return lax.dot_general(a, b, (((1,), (1,)), ((), ())), preferred_element_type=F32)


def scan_kernel(*refs):
    act_own, act_y, halo_a, halo_b, swapped = refs[:5]
    units, refs = refs[5:13], refs[13:]
    prm, heads, refs = refs[0], refs[1], refs[2:]
    xs, maps, sizes, sums, starts, act, kept, given = refs[:8]
    weight, proj, ends = refs[8:]
    z, _, c, _, _, t = place()
    weight[CONVED + HEADS :, :] = jnp.zeros((WA - CONVED - HEADS, D), BF16)
    for n, (unit, f) in enumerate(zip(units, weight_rows())):
        lanes = pl.ds(pl.multiple_of(128 * f, 128), 128)
        weight[:OWN, lanes] = unit[:OWN, :]
        weight[pl.ds(pl.multiple_of(OWN + STATE * c, STATE), STATE), lanes] = unit[OWN : OWN + STATE, :]
        weight[pl.ds(pl.multiple_of(OWN + STATE * (1 - c), STATE), STATE), lanes] = swapped[
            4 * ROWS + HALO :, 128 * n : 128 * n + 128
        ]
        weight[CONVED : CONVED + HEADS, lanes] = unit[OWN + STATE :, :]
    place_act(act, ((act_own, 0), (act_y, 0), (swapped, 0), (swapped, 2 * ROWS)))
    near = halo_a[...] + halo_b[...]
    far = swapped[4 * ROWS : 4 * ROWS + HALO, :]
    act[0, :HALO, :] = jnp.where(c == 1, near, far)
    act[1, :HALO, :] = jnp.where(c == 1, far, near)

    choose = ones_at(iota2((MINE, HEADS), 1) == 4 * iota2((MINE, HEADS), 0) + t).astype(BF16)

    def one_strand(strand, _):
        proj[...] = times_turned(act[strand], weight[...]).astype(BF16).astype(F32)
        turned = []
        for g in range(GROUPS):
            steps = proj[HALO + GROUP * g : HALO + GROUP * g + GROUP, CONVED:].T[:HEADS].astype(BF16)
            turned.append(jnp.dot(choose, steps, preferred_element_type=F32))
        raw = jnp.concatenate(turned, axis=0) + jnp.concatenate([heads[0]] * GROUPS, axis=0)
        size = jnp.maximum(raw, 0.0) + jnp.log1p(jnp.exp(-jnp.abs(raw)))
        decay = -size * jnp.concatenate([heads[1]] * GROUPS, axis=0)
        cumulated = running_sum(decay)
        sizes[strand] = size
        sums[strand] = cumulated
        state = jnp.zeros((STATE, OWN), F32)
        total = jnp.zeros((MINE, 1), F32)
        for g in range(GROUPS):
            rows = slice(GROUP * g, GROUP * g + GROUP)
            for j in range(6):
                cols = slice(128 * j, 128 * j + 128)
                first = HALO - 3 + GROUP * g
                acc = prm[4:5, cols] + prm[0:1, cols] * proj[first : first + GROUP, cols]
                for k in range(1, CONV):
                    acc = acc + prm[k : k + 1, cols] * proj[first + k : first + k + GROUP, cols]
                half = 0.5 * acc
                done = (half + half * jnp.tanh(half)).astype(BF16)
                if j < 4:
                    xs[strand, rows, cols] = done
                else:
                    maps[strand, rows, 128 * (j - 4) : 128 * (j - 4) + 128] = done
            part = slice(MINE * g, MINE * g + MINE)
            last = cumulated[part, GROUP - 1 :]
            total = total + last
            remaining = spread_columns(jnp.exp(last - cumulated[part]) * size[part])
            weighted = (xs[strand, rows, :].astype(F32) * remaining).astype(BF16)
            starts[strand, g] = state.astype(BF16)
            added = lax.dot_general(
                maps[strand, rows, :STATE], weighted, (((0,), (0,)), ((), ())), preferred_element_type=F32
            )
            state = state * spread_row(jnp.exp(last)) + added
        ends[strand, :STATE, :] = state.astype(BF16)
        hi, lo = hi_lo(spread_row(total))
        line = iota2((HALO, OWN), 0)
        ends[strand, STATE:, :] = jnp.where(line == 0, hi, jnp.where(line == 1, lo, 0.0)).astype(BF16)
        return 0

    lax.fori_loop(0, 2, one_strand, 0)
    role = chain(z)
    kept[...] = ends[role]
    given[...] = ends[1 - role]


def chain(z):
    return 1 - lax.rem(z, 2)


def decay_of(ref):
    rows = ref[STATE:, :].astype(F32)
    return rows[0:1] + rows[1:2]


def pair_state(kept, mate, out):
    decay = decay_of(kept)
    out[:STATE, :] = (kept[:STATE, :].astype(F32) + jnp.exp(decay) * mate[:STATE, :].astype(F32)).astype(BF16)
    hi, lo = hi_lo(decay + decay_of(mate))
    line = iota2((HALO, OWN), 0)
    out[STATE:, :] = jnp.where(line == 0, hi, jnp.where(line == 1, lo, 0.0)).astype(BF16)


def earlier_pairs(*refs):
    *pairs, out = refs
    total = jnp.zeros((STATE, OWN), F32)
    gone = jnp.zeros((1, OWN), F32)
    for pair in pairs:
        total = total + jnp.exp(gone) * pair[:STATE, :].astype(F32)
        gone = gone + decay_of(pair)
    out[...] = total.astype(BF16)


def local_kernel(*refs):
    xs, maps, sizes, sums, starts, _, local, carry = refs
    causal = ones_at(iota2((GROUP, GROUP), 0) >= iota2((GROUP, GROUP), 1))
    left = iota2((GROUP, 128), 1) < HEADDIM

    def one_strand(strand, _):
        def one_group(g, before):
            rows = pl.ds(pl.multiple_of(GROUP * g, GROUP), GROUP)
            part = pl.ds(pl.multiple_of(MINE * g, MINE), MINE)
            size = sizes[strand, part, :]
            cumulated = sums[strand, part, :]
            columns = jnp.concatenate([cumulated, jnp.zeros((GROUP - MINE, GROUP), F32)], axis=0).T
            in_map = maps[strand, rows, :STATE]
            out_map = maps[strand, rows, STATE:]
            affinity = lax.dot_general(
                out_map, in_map, (((1,), (1,)), ((), ())), preferred_element_type=F32
            ) * causal
            parts = []
            for pair in range(4):
                mixes = []
                for h in (2 * pair, 2 * pair + 1):
                    gap = jnp.minimum(columns[:, h : h + 1] - cumulated[h : h + 1, :], 0.0)
                    mixes.append((affinity * jnp.exp(gap) * size[h : h + 1, :]).astype(BF16))
                x = xs[strand, rows, 128 * pair : 128 * pair + 128]
                zero = jnp.zeros_like(x)
                tall = jnp.concatenate([jnp.where(left, x, zero), jnp.where(left, zero, x)], axis=0)
                parts.append(jnp.dot(jnp.concatenate(mixes, axis=1), tall, preferred_element_type=F32))
            within = jnp.concatenate(parts, axis=1)
            grown = spread_columns(jnp.exp(cumulated))
            local[strand, rows, :] = within + jnp.dot(out_map, starts[strand, g], preferred_element_type=F32) * grown
            carry[strand, rows, :] = grown * spread_row(jnp.exp(before))
            return before + cumulated[:, GROUP - 1 :]

        lax.fori_loop(0, GROUPS, one_group, jnp.zeros((MINE, 1), F32))
        return 0

    lax.fori_loop(0, 2, one_strand, 0)


def gate_kernel(act, *refs):
    received, refs = refs[:4], refs[4:]
    gate, out_weight, weight = refs
    _, _, _, yh, x, _ = place()
    units = []
    for k, unit in enumerate(received):
        for n, which in enumerate((yh, 1 - yh)):
            units.append((unit, LATE * n, which * 4 + lax.rem(x - k + 4, 4)))
    for unit, first, f in units:
        lanes = pl.ds(pl.multiple_of(128 * f, 128), 128)
        for j in range(MINE):
            weight[64 * j : 64 * j + 64, lanes] = unit[first : first + 64, 128 * j : 128 * j + 128]
        rows = pl.ds(pl.multiple_of(64 * f, 64), 64)
        for half in range(2):
            out_weight[half, rows, :] = unit[first + 64 : first + 128, 512 * half : 512 * half + 512]
    for strand in range(2):
        half = 0.5 * times_turned(act[strand, HALO:, :], weight[...]).astype(BF16).astype(F32)
        gate[strand] = half + half * jnp.tanh(half)


def half_rows(own):
    _, yl, _, _, _, _ = place()
    y = yl if own else 1 - yl
    return 256 * y, 256 * (1 - y)


def project_half(own, weight, entering, prm, maps, local, carry, gate, keep, give, normed):
    _, _, c, _, _, _ = place()
    gain = prm[5:6, :OWN]
    tails = []
    for strand, first in enumerate(half_rows(own)):
        for b in range(2):
            rows = pl.ds(pl.multiple_of(first + ROWS * b, ROWS), ROWS)
            held = jnp.dot(maps[strand, rows, STATE:], entering[strand], preferred_element_type=F32)
            gated = (local[strand, rows, :] + held * carry[strand, rows, :]) * gate[strand, rows, :]
            squared = gated * gated
            folded = (squared[:, :128] + squared[:, 128:256]) + (squared[:, 256:384] + squared[:, 384:])
            tails.append(jnp.sum(folded.T, axis=0, keepdims=True))
            normed[2 * strand + b] = (gated * gain).astype(BF16)
    line = iota2((HALO, ROWS), 0)
    for ref, core in ((keep, c), (give, 1 - c)):
        for strand in range(2):
            b = core if strand == 0 else 1 - core
            for half in range(2):
                ref[ROWS * strand : ROWS * strand + ROWS, 512 * half : 512 * half + 512] = jnp.dot(
                    normed[2 * strand + b], weight[half], preferred_element_type=F32
                ).astype(BF16)
            hi, lo = hi_lo(jnp.where(b == 0, tails[2 * strand], tails[2 * strand + 1]))
            tail = jnp.where(line == 0, hi, jnp.where(line == 1, lo, 0.0))
            ref[2 * ROWS :, ROWS * strand : ROWS * strand + ROWS] = tail.astype(BF16)
        ref[2 * ROWS :, 2 * ROWS :] = jnp.zeros((HALO, D - 2 * ROWS), BF16)


def first_half(*refs):
    mate, entered, mate_entered, refs = refs[0], refs[1], refs[2], refs[3:]
    weight, prm, maps, local, carry, gate, entering, keep, give, normed = refs
    z, _, _, _, _, _ = place()
    role = chain(z)
    entering[role] = (
        mate[:STATE, :].astype(F32) + jnp.exp(decay_of(mate)) * entered[...].astype(F32)
    ).astype(BF16)
    entering[1 - role] = mate_entered[...]
    project_half(False, weight, entering, prm, maps, local, carry, gate, keep, give, normed)


def second_half(weight, entering, prm, maps, local, carry, gate, keep, give, normed):
    project_half(True, weight, entering, prm, maps, local, carry, gate, keep, give, normed)


def pair_sum(mine, came, second, out):
    main = mine[: 2 * ROWS, :].astype(F32) + came[: 2 * ROWS, :].astype(F32)
    out[: 2 * ROWS, :] = main.astype(BF16)
    tail = mine[2 * ROWS :, :].astype(F32) + came[2 * ROWS :, :].astype(F32)
    hi, lo = hi_lo(tail[0:1] + tail[1:2])
    line = iota2((HALO, D), 0)
    out[2 * ROWS :, :] = jnp.where(line == 0, hi, jnp.where(line == 1, lo, 0.0)).astype(BF16)


def last_kernel(mine, came, far, out):
    def tail(ref):
        rows = ref[2 * ROWS :, :].astype(F32)
        return rows[0:1] + rows[1:2]

    squares = tail(mine) + tail(came) + tail(far)
    diagonal = iota2((ROWS, ROWS), 0) == iota2((ROWS, ROWS), 1)
    for strand in range(2):
        rows = slice(ROWS * strand, ROWS * strand + ROWS)
        mean = jnp.sum(jnp.where(diagonal, squares[:, rows], 0.0), axis=1, keepdims=True) * (1.0 / E)
        main = mine[rows, :].astype(F32) + came[rows, :].astype(F32) + far[rows, :].astype(F32)
        block = (main * lax.rsqrt(mean + 1e-05)).astype(BF16)
        if strand:
            block = flipped(block)
        out[:, D * strand : D * strand + D] = block


def swap_core(value):
    return move(value, lambda z, yl, c, yh, x: dict(c=1 - c))


def swap_y(value):
    return move(value, lambda z, yl, c, yh, x: dict(yl=1 - yl))


def swap_diagonal(value, k=0):
    return move(value, lambda z, yl, c, yh, x: dict(yl=1 - yl, yh=1 - yh, x=(x + k) % 4))


def along_x(value, k):
    return move(value, lambda z, yl, c, yh, x: dict(x=(x + k) % 4))


def pair_step(m):
    def to(z, yl, c, yh, x):
        target = z + 2 * m if z % 2 else z - 2 * m
        return dict(z=target) if 0 <= target < Z else None

    return to


def halo_step(same):
    def to(z, yl, c, yh, x):
        t = 2 * yl + c
        if t == 3 and z < Z - 1:
            return dict(z=z + 1, yl=1 if same else 0)
        if t == 0 and z > 0:
            return dict(z=z - 1, yl=0 if same else 1)
        return None

    return to


def body(hidden, tokens, base_bias, in_weight, conv_weight, conv_bias, dt_bias, decay_rate, norm_gain, out_weight):
    act, halo, ua, ua_other, ub, ub_other = call(
        start_kernel,
        "start_kernel",
        [shape(2 * ROWS, D), shape(HALO, D)] + [shape(UNIT, 128)] * 2 + [shape(LATE, D)] * 2,
        [ANY] * 5,
        tuple(
            pltpu.with_memory_space_constraint(value, pltpu.HBM)
            for value in (hidden[0], tokens, base_bias, in_weight.T, out_weight)
        ),
        scratch=[
            pltpu.VMEM((ROWS, 2 * D), BF16),
            pltpu.VMEM((1, ROWS), jnp.int32),
            pltpu.VMEM((5, 2 * D), BF16),
            pltpu.VMEM((WIDE, ROWS), BF16),
            pltpu.VMEM((2 * ROWS, D), BF16),
            pltpu.SemaphoreType.DMA((6,)),
        ],
        mb=16,
    )
    act_y = swap_y(act)
    far = swap_diagonal(ua_other)
    own_1, own_3 = along_x(ua, 1), along_x(ua, 3)
    halo_a = move(halo, halo_step(True))
    halo, ub_other, ua_late = call(
        hold,
        "hold",
        [shape(HALO, D), shape(LATE, D), shape(UNIT, 128)],
        [VMEM] * 4,
        (halo, ub_other, ua, far),
        mb=8,
    )
    own_2 = along_x(ua_late, 2)
    far_1, far_3, far_2 = along_x(far, 1), along_x(far, 3), along_x(far, 2)
    units = (ua, own_1, own_2, own_3, far, far_1, far_2, far_3)
    halo_b = move(halo, halo_step(False))
    ub_far = swap_diagonal(ub_other)
    payload, late = call(
        pack_core,
        "pack_core",
        [shape(PAYLOAD, D), shape(2 * LATE, D)],
        [VMEM] * 14,
        (act, act_y, halo_a, halo_b, ub, ub_far, *units),
        mb=12,
    )
    swapped = swap_core(payload)
    late = (late, *[along_x(late, k) for k in (1, 2, 3)])
    prm, heads = call(
        pack_params,
        "pack_params",
        [shape(8, CONVED, dtype=F32), shape(2, MINE, 128, dtype=F32)],
        [VMEM] * 5,
        (conv_weight, conv_bias[None], dt_bias[None], decay_rate[None], norm_gain[None]),
        scratch=[pltpu.VMEM((8, E), F32)],
        mb=12,
    )
    xs, maps, sizes, sums, starts, act, kept, given = call(
        scan_kernel,
        "scan_kernel",
        [
            shape(2, SPAN, OWN),
            shape(2, SPAN, 2 * STATE),
            shape(2, MINE * GROUPS, GROUP, dtype=F32),
            shape(2, MINE * GROUPS, GROUP, dtype=F32),
            shape(2, GROUPS, STATE, OWN),
            shape(2, PAD, D),
        ]
        + [shape(STATE + HALO, OWN)] * 2,
        [VMEM] * 15,
        (act, act_y, halo_a, halo_b, swapped, *units, prm, heads),
        scratch=[
            pltpu.VMEM((WA, D), BF16),
            pltpu.VMEM((PAD, WA), F32),
            pltpu.VMEM((2, STATE + HALO, OWN), BF16),
        ],
        mb=24,
        flops=2 * 1056 * D * WA,
        bytes_accessed=8 << 20,
    )
    mate = move(given, lambda z, yl, c, yh, x: dict(z=z ^ 1))
    pair = call(pair_state, "pair_state", shape(STATE + HALO, OWN), [VMEM] * 2, (kept, mate), mb=8)
    earlier = [move(pair, pair_step(m)) for m in (1, 2, 3)]
    entered = call(earlier_pairs, "earlier_pairs", shape(STATE, OWN), [VMEM] * 3, earlier, mb=8)
    mate_entered = move(entered, lambda z, yl, c, yh, x: dict(z=z ^ 1))
    local, carry = call(
        local_kernel,
        "local_kernel",
        [shape(2, SPAN, OWN, dtype=F32)] * 2,
        [VMEM] * 6,
        (xs, maps, sizes, sums, starts, pair),
        mb=16,
        flops=8 * 1024 * D * OWN,
        bytes_accessed=16 << 20,
    )
    gate, weight = call(
        gate_kernel,
        "gate_kernel",
        [shape(2, SPAN, OWN, dtype=F32), shape(2, OWN, 512)],
        [VMEM] * (1 + len(late)),
        (act, *late),
        scratch=[pltpu.VMEM((OWN, D), BF16)],
        mb=16,
        flops=2 * 1024 * D * OWN,
        bytes_accessed=8 << 20,
    )
    half_out = [shape(2 * ROWS + HALO, D)] * 2
    half_scratch = [pltpu.VMEM((4, ROWS, OWN), BF16)]
    entering, keep, give = call(
        first_half,
        "first_half",
        [shape(2, STATE, OWN)] + half_out,
        [VMEM] * 9,
        (mate, entered, mate_entered, weight, prm, maps, local, carry, gate),
        scratch=half_scratch,
        mb=16,
        flops=1024 * D * OWN,
        bytes_accessed=4 << 20,
    )
    keep_2, give_2 = call(
        second_half,
        "second_half",
        half_out,
        [VMEM] * 7,
        (weight, entering, prm, maps, local, carry, gate),
        scratch=half_scratch,
        mb=16,
        flops=1024 * D * OWN,
        bytes_accessed=4 << 20,
    )
    part = call(
        pair_sum, "pair_sum", shape(2 * ROWS + HALO, D), [VMEM] * 3, (keep, swap_core(give), keep_2), mb=8
    )
    far_part = swap_y(part)
    out = call(last_kernel, "last_kernel", shape(ROWS, 2 * D), [VMEM] * 3, (keep_2, swap_core(give_2), far_part), mb=8)
    return out[None]


def solution(mesh):
    placed = (
        P("fsdp", "seq", None),
        P("fsdp", "seq"),
        P(),
        P("fsdp", None),
        P(),
        P(),
        P(),
        P(),
        P(),
        P("fsdp", None),
    )
    return jax.shard_map(
        body, mesh=mesh, in_specs=placed, out_specs=P("fsdp", "seq", None), check_vma=False
    )
```

```python
import jax
import jax.numpy as jnp
from jax import lax
from jax.experimental import pallas as pl
from jax.experimental.pallas import tpu as pltpu
from jax.sharding import PartitionSpec as P

D = 1024
HEADS = 32
HEADDIM = 64
STATE = 128
CONV = 4
GROUP = 128
E = 2048
WIDE = 4384
ROWS = 128
SPAN = 512
GROUPS = SPAN // GROUP
OWN = 512
MINE = 8
HALO = 16
PAD = HALO + SPAN
CONVED = OWN + 2 * STATE
WA = CONVED + 128
UNIT = OWN + STATE + HEADS
LATE = 2 * OWN
Z = 8
PAYLOAD = 4 * ROWS + HALO + STATE

F32 = jnp.float32
BF16 = jnp.bfloat16
EXACT = lax.Precision.HIGHEST
ANY = pl.BlockSpec(memory_space=pl.ANY)
VMEM = pl.BlockSpec(memory_space=pltpu.VMEM)


def place():
    s, f = lax.axis_index("seq"), lax.axis_index("fsdp")
    t = lax.rem(s, 4)
    return s // 4, t // 2, lax.rem(t, 2), f // 4, lax.rem(f, 4), t


def move(value, to):
    pairs = []
    for s in range(32):
        for f in range(8):
            here = dict(z=s // 4, yl=(s // 2) % 2, c=s % 2, yh=f // 4, x=f % 4)
            change = to(**here)
            if change is None:
                continue
            there = {**here, **change}
            target = (there["z"] * 4 + there["yl"] * 2 + there["c"]) * 8 + there["yh"] * 4 + there["x"]
            pairs.append((s * 8 + f, target))
    return lax.ppermute(value, ("seq", "fsdp"), pairs)


def shape(*dims, dtype=BF16):
    return jax.ShapeDtypeStruct(dims, dtype)


def call(kernel, name, outs, ins, operands, scratch=(), mb=48, flops=0, bytes_accessed=0, out_specs=None):
    return pl.pallas_call(
        kernel,
        out_shape=outs,
        in_specs=ins,
        out_specs=jax.tree.map(lambda _: VMEM, outs) if out_specs is None else out_specs,
        scratch_shapes=scratch,
        name=name,
        compiler_params=pltpu.CompilerParams(vmem_limit_bytes=mb << 20),
        cost_estimate=pl.CostEstimate(flops=flops, bytes_accessed=bytes_accessed, transcendentals=0),
    )(*operands)


def iota2(dims, dim):
    return lax.broadcasted_iota(jnp.int32, dims, dim)


def ones_at(where):
    return jnp.where(where, 1.0, 0.0)


def anti_identity():
    return ones_at(iota2((128, 128), 0) + iota2((128, 128), 1) == 127).astype(BF16)


def flipped(block):
    anti = anti_identity()
    rows = jnp.dot(anti, block, preferred_element_type=F32).astype(BF16)
    parts = [
        jnp.dot(rows[:, 128 * j : 128 * j + 128], anti, preferred_element_type=F32).astype(BF16)
        for j in range(D // 128)
    ]
    return jnp.concatenate(parts[::-1], axis=1)


def head_pick():
    _, _, _, _, _, t = place()
    row, col = iota2((512, 128), 0), iota2((512, 128), 1)
    return ones_at(row == 256 * (col // 64) + 64 * t + lax.rem(col, 64))


def start_kernel(hidden, tokens, base_bias, iw, ow, act, ua, ub, other, rows_in, ids_in, bias_in, iw_in, ow_in, sem):
    _, yl, c, _, _, t = place()
    copies = [
        pltpu.make_async_copy(tokens, ids_in, sem.at[0]),
        pltpu.make_async_copy(base_bias, bias_in, sem.at[1]),
        pltpu.make_async_copy(hidden, rows_in, sem.at[2]),
        pltpu.make_async_copy(iw.at[pl.ds(E, WIDE - E)], iw_in.at[pl.ds(E, WIDE - E)], sem.at[3]),
        pltpu.make_async_copy(iw.at[pl.ds(0, E)], iw_in.at[pl.ds(0, E)], sem.at[4]),
        pltpu.make_async_copy(ow, ow_in, sem.at[5]),
    ]
    for copy in copies:
        copy.start()
    for copy in copies[:3]:
        copy.wait()
    ids = ids_in[...]
    letter = iota2((5, ROWS), 0)
    paired = jnp.where(ids == 4, 4, 3 - ids)
    for strand, chosen in ((0, ids), (1, paired)):
        onehot = ones_at(letter == chosen).astype(BF16)
        bias = lax.dot_general(
            onehot, bias_in[:, D * strand : D * strand + D], (((0,), (0,)), ((), ())), preferred_element_type=F32
        )
        block = (rows_in[:, D * strand : D * strand + D].astype(F32) + bias).astype(BF16)
        if strand:
            block = flipped(block)
        act[ROWS * strand : ROWS * strand + ROWS, :] = block
    for copy in copies[3:]:
        copy.wait()
    for early, first, late, second, which in ((ua, 0, ub, 0, t), (other, 0, other, UNIT, (1 - yl) * 2 + c)):
        for j in range(MINE):
            row = pl.multiple_of(256 * j + 64 * which, 64)
            early[first + 64 * j : first + 64 * j + 64, :] = iw_in[pl.ds(E + row, 64), :]
            late[second + 64 * j : second + 64 * j + 64, :] = iw_in[pl.ds(row, 64), :]
            out_rows = ow_in[pl.ds(pl.multiple_of(64 * which, 64), 64), 128 * j : 128 * j + 128]
            late[second + OWN + 64 * j : second + OWN + 64 * j + 64, :] = out_rows
        shared = iw_in[pl.ds(pl.multiple_of(2 * E + STATE * c, STATE), STATE), :]
        early[first + OWN : first + OWN + STATE, :] = shared
        early[first + OWN + STATE : first + UNIT, :] = iw_in[2 * E + 2 * STATE :, :]


def split_far(both, prm, far):
    far[...] = both[:UNIT, :]


def choose_halo(act, act_y, far, halo, far_out):
    _, yl, c, _, _, _ = place()
    forward = jnp.where(yl == 1, act[ROWS - HALO : ROWS, :], act_y[ROWS - HALO : ROWS, :])
    reverse = jnp.where(yl == 0, act[2 * ROWS - HALO :, :], act_y[2 * ROWS - HALO :, :])
    halo[...] = jnp.where(c == 1, forward, reverse)
    far_out[...] = far[...]


def pack_params(cw, cb, dtb, rate, gain, prm, heads, stack):
    _, _, _, _, _, t = place()
    pick = head_pick()
    stack[...] = jnp.zeros_like(stack)
    stack[0:4, :] = cw[:, :E]
    stack[4:5, :] = cb[:, :E]
    stack[5:6, :] = gain[...]
    prm[...] = jnp.zeros_like(prm)
    for j in range(4):
        prm[:, 128 * j : 128 * j + 128] = jnp.dot(
            stack[:, 512 * j : 512 * j + 512], pick, precision=EXACT, preferred_element_type=F32
        )
    prm[0:4, OWN:] = cw[:, E:]
    prm[4:5, OWN:] = cb[:, E:]
    chosen = iota2((MINE, HEADS), 1) == 4 * iota2((MINE, HEADS), 0) + t
    for n, ref in enumerate((dtb, rate)):
        column = jnp.sum(jnp.where(chosen, ref[...], 0.0), axis=1, keepdims=True)
        heads[n] = jnp.broadcast_to(column, (MINE, 128))


def pack_core(*refs):
    act, act_y, halo, ub, both = refs[:5]
    units, out, out_b = refs[5:13], refs[13], refs[14]
    out_b[:LATE, :] = ub[...]
    out_b[LATE:, :] = both[UNIT:, :]
    out[: 2 * ROWS, :] = act[...]
    out[2 * ROWS : 4 * ROWS, :] = act_y[...]
    out[4 * ROWS : 4 * ROWS + HALO, :] = halo[...]
    for n, unit in enumerate(units):
        out[4 * ROWS + HALO :, 128 * n : 128 * n + 128] = unit[OWN : OWN + STATE, :]


def weight_rows():
    _, _, _, yh, x, _ = place()
    return [which * 4 + lax.rem(x - k + 4, 4) for which in (yh, 1 - yh) for k in range(4)]


def place_act(act, blocks):
    _, _, _, _, _, t = place()
    for (ref, first), other in zip(blocks, (0, 2, 1, 3)):
        at = t ^ other
        for strand, row in ((0, at), (1, 3 - at)):
            act[strand, pl.ds(pl.multiple_of(HALO + ROWS * row, 16), ROWS), :] = ref[
                first + ROWS * strand : first + ROWS * strand + ROWS, :
            ]


def spread_heads(count):
    return ones_at(lax.rem(iota2((MINE * count, OWN), 0), MINE) == iota2((MINE * count, OWN), 1) // HEADDIM)


def hi_lo(v):
    hi = v.astype(BF16).astype(F32)
    return hi, v - hi


def spread_columns(rows):
    both = jnp.concatenate(hi_lo(rows), axis=0).astype(BF16)
    return lax.dot_general(
        both, spread_heads(2).astype(BF16), (((0,), (0,)), ((), ())), preferred_element_type=F32
    )


def spread_row(column):
    return jnp.sum(spread_heads(1) * column, axis=0, keepdims=True)


def running_sum(rows):
    count = rows.shape[0]
    hi, rest = hi_lo(rows)
    mid, low = hi_lo(rest)
    upper = ones_at(iota2((GROUP, GROUP), 0) <= iota2((GROUP, GROUP), 1)).astype(BF16)
    pieces = jnp.concatenate([hi, mid, low], axis=0).astype(BF16)
    sums = jnp.dot(pieces, upper, preferred_element_type=F32)
    return sums[:count] + sums[count : 2 * count] + sums[2 * count :]


def times_turned(a, b):
    return lax.dot_general(a, b, (((1,), (1,)), ((), ())), preferred_element_type=F32)


def scan_strand(strand, act, weight, prm, heads, xs, maps, sizes, sums, starts, end, proj):
    _, _, _, _, _, t = place()
    choose = ones_at(iota2((MINE, HEADS), 1) == 4 * iota2((MINE, HEADS), 0) + t).astype(BF16)
    proj[...] = times_turned(act[strand], weight[...]).astype(BF16).astype(F32)
    turned = []
    for g in range(GROUPS):
        steps = proj[HALO + GROUP * g : HALO + GROUP * g + GROUP, CONVED:].T[:HEADS].astype(BF16)
        turned.append(jnp.dot(choose, steps, preferred_element_type=F32))
    raw = jnp.concatenate(turned, axis=0) + jnp.concatenate([heads[0]] * GROUPS, axis=0)
    size = jnp.maximum(raw, 0.0) + jnp.log1p(jnp.exp(-jnp.abs(raw)))
    decay = -size * jnp.concatenate([heads[1]] * GROUPS, axis=0)
    cumulated = running_sum(decay)
    sizes[...] = size
    sums[...] = cumulated
    state = jnp.zeros((STATE, OWN), F32)
    total = jnp.zeros((MINE, 1), F32)
    for g in range(GROUPS):
        rows = slice(GROUP * g, GROUP * g + GROUP)
        for j in range(6):
            cols = slice(128 * j, 128 * j + 128)
            first = HALO - 3 + GROUP * g
            acc = prm[4:5, cols] + prm[0:1, cols] * proj[first : first + GROUP, cols]
            for k in range(1, CONV):
                acc = acc + prm[k : k + 1, cols] * proj[first + k : first + k + GROUP, cols]
            half = 0.5 * acc
            done = (half + half * jnp.tanh(half)).astype(BF16)
            if j < 4:
                xs[rows, cols] = done
            else:
                maps[rows, 128 * (j - 4) : 128 * (j - 4) + 128] = done
        part = slice(MINE * g, MINE * g + MINE)
        last = cumulated[part, GROUP - 1 :]
        total = total + last
        remaining = spread_columns(jnp.exp(last - cumulated[part]) * size[part])
        weighted = (xs[rows, :].astype(F32) * remaining).astype(BF16)
        starts[g] = state.astype(BF16)
        added = lax.dot_general(
            maps[rows, :STATE], weighted, (((0,), (0,)), ((), ())), preferred_element_type=F32
        )
        state = state * spread_row(jnp.exp(last)) + added
    end[:STATE, :] = state.astype(BF16)
    hi, lo = hi_lo(spread_row(total))
    line = iota2((HALO, OWN), 0)
    end[STATE:, :] = jnp.where(line == 0, hi, jnp.where(line == 1, lo, 0.0)).astype(BF16)


def first_scan(*refs):
    act_own, act_y, halo, swapped = refs[:4]
    units, refs = refs[4:12], refs[12:]
    prm, heads, xs, maps, sizes, sums, starts, act, weight, end, proj = refs
    z, _, c, _, _, _ = place()
    weight[CONVED + HEADS :, :] = jnp.zeros((WA - CONVED - HEADS, D), BF16)
    for n, (unit, f) in enumerate(zip(units, weight_rows())):
        lanes = pl.ds(pl.multiple_of(128 * f, 128), 128)
        weight[:OWN, lanes] = unit[:OWN, :]
        weight[pl.ds(pl.multiple_of(OWN + STATE * c, STATE), STATE), lanes] = unit[OWN : OWN + STATE, :]
        weight[pl.ds(pl.multiple_of(OWN + STATE * (1 - c), STATE), STATE), lanes] = swapped[
            4 * ROWS + HALO :, 128 * n : 128 * n + 128
        ]
        weight[CONVED : CONVED + HEADS, lanes] = unit[OWN + STATE :, :]
    place_act(act, ((act_own, 0), (act_y, 0), (swapped, 0), (swapped, 2 * ROWS)))
    near = halo[...]
    far = swapped[4 * ROWS : 4 * ROWS + HALO, :]
    act[0, :HALO, :] = jnp.where(c == 1, near, far)
    act[1, :HALO, :] = jnp.where(c == 1, far, near)
    scan_strand(1 - chain(z), act, weight, prm, heads, xs, maps, sizes, sums, starts, end, proj)


def second_scan(act, weight, prm, heads, xs, maps, sizes, sums, starts, end, proj):
    z, _, _, _, _, _ = place()
    scan_strand(chain(z), act, weight, prm, heads, xs, maps, sizes, sums, starts, end, proj)


def chain(z):
    return 1 - lax.rem(z, 2)


def decay_of(ref):
    rows = ref[STATE:, :].astype(F32)
    return rows[0:1] + rows[1:2]


def pair_state(kept, mate, out):
    decay = decay_of(kept)
    out[:STATE, :] = (kept[:STATE, :].astype(F32) + jnp.exp(decay) * mate[:STATE, :].astype(F32)).astype(BF16)
    hi, lo = hi_lo(decay + decay_of(mate))
    line = iota2((HALO, OWN), 0)
    out[STATE:, :] = jnp.where(line == 0, hi, jnp.where(line == 1, lo, 0.0)).astype(BF16)


def earlier_pairs(*refs):
    *pairs, out = refs
    total = jnp.zeros((STATE, OWN), F32)
    gone = jnp.zeros((1, OWN), F32)
    for pair in pairs:
        total = total + jnp.exp(gone) * pair[:STATE, :].astype(F32)
        gone = gone + decay_of(pair)
    out[...] = total.astype(BF16)


def local_kernel(*refs):
    scans, refs = (refs[:5], refs[5:10]), refs[11:]
    local, carry, out_maps = refs
    z, _, _, _, _, _ = place()
    causal = ones_at(iota2((GROUP, GROUP), 0) >= iota2((GROUP, GROUP), 1))
    left = iota2((GROUP, 128), 1) < HEADDIM
    for strand, (xs, maps, sizes, sums, starts) in zip((1 - chain(z), chain(z)), scans):
        out_maps[strand] = maps[:, STATE:]

        def one_group(g, before, strand=strand, xs=xs, maps=maps, sizes=sizes, sums=sums, starts=starts):
            rows = pl.ds(pl.multiple_of(GROUP * g, GROUP), GROUP)
            part = pl.ds(pl.multiple_of(MINE * g, MINE), MINE)
            size = sizes[part, :]
            cumulated = sums[part, :]
            columns = jnp.concatenate([cumulated, jnp.zeros((GROUP - MINE, GROUP), F32)], axis=0).T
            in_map = maps[rows, :STATE]
            out_map = maps[rows, STATE:]
            affinity = times_turned(out_map, in_map) * causal
            parts = []
            for pair in range(4):
                mixes = []
                for h in (2 * pair, 2 * pair + 1):
                    gap = jnp.minimum(columns[:, h : h + 1] - cumulated[h : h + 1, :], 0.0)
                    mixes.append((affinity * jnp.exp(gap) * size[h : h + 1, :]).astype(BF16))
                x = xs[rows, 128 * pair : 128 * pair + 128]
                zero = jnp.zeros_like(x)
                tall = jnp.concatenate([jnp.where(left, x, zero), jnp.where(left, zero, x)], axis=0)
                parts.append(jnp.dot(jnp.concatenate(mixes, axis=1), tall, preferred_element_type=F32))
            within = jnp.concatenate(parts, axis=1)
            grown = spread_columns(jnp.exp(cumulated))
            local[strand, rows, :] = within + jnp.dot(out_map, starts[g], preferred_element_type=F32) * grown
            carry[strand, rows, :] = grown * spread_row(jnp.exp(before))
            return before + cumulated[:, GROUP - 1 :]

        lax.fori_loop(0, GROUPS, one_group, jnp.zeros((MINE, 1), F32))


def gate_kernel(act, *refs):
    received, refs = refs[:4], refs[4:]
    gate, out_weight, weight = refs
    _, _, _, yh, x, _ = place()
    units = []
    for k, unit in enumerate(received):
        for n, which in enumerate((yh, 1 - yh)):
            units.append((unit, LATE * n, which * 4 + lax.rem(x - k + 4, 4)))
    for unit, first, f in units:
        lanes = pl.ds(pl.multiple_of(128 * f, 128), 128)
        weight[:, lanes] = unit[first : first + OWN, :]
        rows = pl.ds(pl.multiple_of(64 * f, 64), 64)
        for j in range(8):
            line = first + OWN + 64 * j
            out_weight[j // 4, rows, 128 * (j % 4) : 128 * (j % 4) + 128] = unit[line : line + 64, :]
    for strand in range(2):
        half = 0.5 * times_turned(act[strand, HALO:, :], weight[...]).astype(BF16).astype(F32)
        gate[strand] = half + half * jnp.tanh(half)


def half_rows(own):
    _, yl, _, _, _, _ = place()
    y = yl if own else 1 - yl
    return 256 * y, 256 * (1 - y)


def project_half(own, weight, entering, prm, maps, local, carry, gate, keep, give, normed):
    _, _, c, _, _, _ = place()
    gain = prm[5:6, :OWN]
    tails = []
    for strand, first in enumerate(half_rows(own)):
        for b in range(2):
            rows = pl.ds(pl.multiple_of(first + ROWS * b, ROWS), ROWS)
            held = jnp.dot(maps[strand, rows, :], entering[strand], preferred_element_type=F32)
            gated = (local[strand, rows, :] + held * carry[strand, rows, :]) * gate[strand, rows, :]
            squared = gated * gated
            folded = (squared[:, :128] + squared[:, 128:256]) + (squared[:, 256:384] + squared[:, 384:])
            tails.append(jnp.sum(folded.T, axis=0, keepdims=True))
            normed[2 * strand + b] = (gated * gain).astype(BF16)
    line = iota2((HALO, ROWS), 0)
    for ref, core in ((keep, c), (give, 1 - c)):
        for strand in range(2):
            b = core if strand == 0 else 1 - core
            for half in range(2):
                ref[ROWS * strand : ROWS * strand + ROWS, 512 * half : 512 * half + 512] = jnp.dot(
                    normed[2 * strand + b], weight[half], preferred_element_type=F32
                ).astype(BF16)
            hi, lo = hi_lo(jnp.where(b == 0, tails[2 * strand], tails[2 * strand + 1]))
            tail = jnp.where(line == 0, hi, jnp.where(line == 1, lo, 0.0))
            ref[2 * ROWS :, ROWS * strand : ROWS * strand + ROWS] = tail.astype(BF16)
        ref[2 * ROWS :, 2 * ROWS :] = jnp.zeros((HALO, D - 2 * ROWS), BF16)


def first_half(*refs):
    mate, entered, mate_entered, refs = refs[0], refs[1], refs[2], refs[3:]
    weight, prm, maps, local, carry, gate, entering, keep, give, normed = refs
    z, _, _, _, _, _ = place()
    role = chain(z)
    entering[role] = (
        mate[:STATE, :].astype(F32) + jnp.exp(decay_of(mate)) * entered[...].astype(F32)
    ).astype(BF16)
    entering[1 - role] = mate_entered[...]
    project_half(False, weight, entering, prm, maps, local, carry, gate, keep, give, normed)


def second_half(weight, entering, prm, maps, local, carry, gate, keep, give, normed):
    project_half(True, weight, entering, prm, maps, local, carry, gate, keep, give, normed)


def pair_sum(mine, came, second, out):
    main = mine[: 2 * ROWS, :].astype(F32) + came[: 2 * ROWS, :].astype(F32)
    out[: 2 * ROWS, :] = main.astype(BF16)
    tail = mine[2 * ROWS :, :].astype(F32) + came[2 * ROWS :, :].astype(F32)
    hi, lo = hi_lo(tail[0:1] + tail[1:2])
    line = iota2((HALO, D), 0)
    out[2 * ROWS :, :] = jnp.where(line == 0, hi, jnp.where(line == 1, lo, 0.0)).astype(BF16)


def last_kernel(mine, came, far, out):
    def tail(ref):
        rows = ref[2 * ROWS :, :].astype(F32)
        return rows[0:1] + rows[1:2]

    squares = tail(mine) + tail(came) + tail(far)
    diagonal = iota2((ROWS, ROWS), 0) == iota2((ROWS, ROWS), 1)
    for strand in range(2):
        rows = slice(ROWS * strand, ROWS * strand + ROWS)
        mean = jnp.sum(jnp.where(diagonal, squares[:, rows], 0.0), axis=1, keepdims=True) * (1.0 / E)
        main = mine[rows, :].astype(F32) + came[rows, :].astype(F32) + far[rows, :].astype(F32)
        block = (main * lax.rsqrt(mean + 1e-05)).astype(BF16)
        if strand:
            block = flipped(block)
        out[:, D * strand : D * strand + D] = block


def swap_core(value):
    return move(value, lambda z, yl, c, yh, x: dict(c=1 - c))


def swap_y(value):
    return move(value, lambda z, yl, c, yh, x: dict(yl=1 - yl))


def swap_diagonal(value, k=0):
    return move(value, lambda z, yl, c, yh, x: dict(yl=1 - yl, yh=1 - yh, x=(x + k) % 4))


def along_x(value, k):
    return move(value, lambda z, yl, c, yh, x: dict(x=(x + k) % 4))


def pair_step(m):
    def to(z, yl, c, yh, x):
        target = z + 2 * m if z % 2 else z - 2 * m
        return dict(z=target) if 0 <= target < Z else None

    return to


def halo_step(z, yl, c, yh, x):
    target = z + 1 if c else z - 1
    return dict(z=target) if 0 <= target < Z else None


def body(hidden, tokens, base_bias, in_weight, conv_weight, conv_bias, dt_bias, decay_rate, norm_gain, out_weight):
    act, ua, ub, other = call(
        start_kernel,
        "start_kernel",
        [shape(2 * ROWS, D), shape(UNIT, 128), shape(LATE, 128), shape(UNIT + LATE, 128)],
        [ANY] * 5,
        tuple(
            pltpu.with_memory_space_constraint(value, pltpu.HBM)
            for value in (hidden[0], tokens, base_bias, in_weight.T, out_weight)
        ),
        scratch=[
            pltpu.VMEM((ROWS, 2 * D), BF16),
            pltpu.VMEM((1, ROWS), jnp.int32),
            pltpu.VMEM((5, 2 * D), BF16),
            pltpu.VMEM((WIDE, ROWS), BF16),
            pltpu.VMEM((2 * ROWS, D), BF16),
            pltpu.SemaphoreType.DMA((6,)),
        ],
        mb=16,
    )
    act_y = swap_y(act)
    both = swap_diagonal(other)
    own_1, own_3, own_2 = along_x(ua, 1), along_x(ua, 3), along_x(ua, 2)
    prm, heads = call(
        pack_params,
        "pack_params",
        [shape(8, CONVED, dtype=F32), shape(2, MINE, 128, dtype=F32)],
        [VMEM] * 5,
        (conv_weight, conv_bias[None], dt_bias[None], decay_rate[None], norm_gain[None]),
        scratch=[pltpu.VMEM((8, E), F32)],
        mb=12,
    )
    far = call(split_far, "split_far", shape(UNIT, 128), [VMEM] * 2, (both, prm), mb=8)
    far_1, far_3 = along_x(far, 1), along_x(far, 3)
    halo, far_late = call(
        choose_halo, "choose_halo", [shape(HALO, D), shape(UNIT, 128)], [VMEM] * 3, (act, act_y, far), mb=8
    )
    halo = move(halo, halo_step)
    far_2 = along_x(far_late, 2)
    units = (ua, own_1, own_2, own_3, far, far_1, far_2, far_3)
    payload, late = call(
        pack_core,
        "pack_core",
        [shape(PAYLOAD, D), shape(2 * LATE, 128)],
        [VMEM] * 13,
        (act, act_y, halo, ub, both, *units),
        mb=12,
    )
    swapped = swap_core(payload)
    late = (late, *[along_x(late, k) for k in (1, 2, 3)])
    scanned = [
        shape(SPAN, OWN),
        shape(SPAN, 2 * STATE),
        shape(MINE * GROUPS, GROUP, dtype=F32),
        shape(MINE * GROUPS, GROUP, dtype=F32),
        shape(GROUPS, STATE, OWN),
    ]
    *first, act, weight, given = call(
        first_scan,
        "first_scan",
        scanned + [shape(2, PAD, D), shape(WA, D), shape(STATE + HALO, OWN)],
        [VMEM] * 14,
        (act, act_y, halo, swapped, *units, prm, heads),
        scratch=[pltpu.VMEM((PAD, WA), F32)],
        mb=20,
        flops=1056 * D * WA,
        bytes_accessed=8 << 20,
    )
    *second, kept = call(
        second_scan,
        "second_scan",
        scanned + [shape(STATE + HALO, OWN)],
        [VMEM] * 4,
        (act, weight, prm, heads),
        scratch=[pltpu.VMEM((PAD, WA), F32)],
        mb=20,
        flops=16 * 1056 * D * WA,
        bytes_accessed=8 << 20,
    )
    mate = move(given, lambda z, yl, c, yh, x: dict(z=z ^ 1))
    pair = call(pair_state, "pair_state", shape(STATE + HALO, OWN), [VMEM] * 2, (kept, mate), mb=8)
    earlier = [move(pair, pair_step(m)) for m in (1, 2, 3)]
    entered = call(earlier_pairs, "earlier_pairs", shape(STATE, OWN), [VMEM] * 3, earlier, mb=8)
    mate_entered = move(entered, lambda z, yl, c, yh, x: dict(z=z ^ 1))
    local, carry, maps = call(
        local_kernel,
        "local_kernel",
        [shape(2, SPAN, OWN, dtype=F32)] * 2 + [shape(2, SPAN, STATE)],
        [VMEM] * 11,
        (*first, *second, pair),
        mb=16,
        flops=8 * 1024 * D * OWN,
        bytes_accessed=16 << 20,
    )
    gate, weight = call(
        gate_kernel,
        "gate_kernel",
        [shape(2, SPAN, OWN, dtype=F32), shape(2, OWN, 512)],
        [VMEM] * (1 + len(late)),
        (act, *late),
        scratch=[pltpu.VMEM((OWN, D), BF16)],
        mb=16,
        flops=2 * 1024 * D * OWN,
        bytes_accessed=8 << 20,
    )
    half_out = [shape(2 * ROWS + HALO, D)] * 2
    half_scratch = [pltpu.VMEM((4, ROWS, OWN), BF16)]
    entering, keep, give = call(
        first_half,
        "first_half",
        [shape(2, STATE, OWN)] + half_out,
        [VMEM] * 9,
        (mate, entered, mate_entered, weight, prm, maps, local, carry, gate),
        scratch=half_scratch,
        mb=16,
        flops=1024 * D * OWN,
        bytes_accessed=4 << 20,
    )
    keep_2, give_2 = call(
        second_half,
        "second_half",
        half_out,
        [VMEM] * 7,
        (weight, entering, prm, maps, local, carry, gate),
        scratch=half_scratch,
        mb=16,
        flops=1024 * D * OWN,
        bytes_accessed=4 << 20,
    )
    part = call(
        pair_sum, "pair_sum", shape(2 * ROWS + HALO, D), [VMEM] * 3, (keep, swap_core(give), keep_2), mb=8
    )
    far_part = swap_y(part)
    out = call(last_kernel, "last_kernel", shape(ROWS, 2 * D), [VMEM] * 3, (keep_2, swap_core(give_2), far_part), mb=8)
    return out[None]


def solution(mesh):
    placed = (
        P("fsdp", "seq", None),
        P("fsdp", "seq"),
        P(),
        P("fsdp", None),
        P(),
        P(),
        P(),
        P(),
        P(),
        P("fsdp", None),
    )
    return jax.shard_map(
        body, mesh=mesh, in_specs=placed, out_specs=P("fsdp", "seq", None), check_vma=False
    )
```

```python
import jax
import jax.numpy as jnp
from jax import lax
from jax.experimental import pallas as pl
from jax.experimental.pallas import tpu as pltpu
from jax.sharding import PartitionSpec as P

D = 1024
HEADS = 32
HEADDIM = 64
STATE = 128
CONV = 4
GROUP = 128
E = 2048
WIDE = 4384
ROWS = 128
SPAN = 512
GROUPS = SPAN // GROUP
OWN = 512
MINE = 8
HALO = 16
PAD = HALO + SPAN
CONVED = OWN + 2 * STATE
WA = CONVED + 128
UNIT = OWN + STATE + HEADS
LATE = 2 * OWN
Z = 8
PAYLOAD = 4 * ROWS + HALO + STATE

F32 = jnp.float32
BF16 = jnp.bfloat16
EXACT = lax.Precision.HIGHEST
ANY = pl.BlockSpec(memory_space=pl.ANY)
VMEM = pl.BlockSpec(memory_space=pltpu.VMEM)


def place():
    s, f = lax.axis_index("seq"), lax.axis_index("fsdp")
    t = lax.rem(s, 4)
    return s // 4, t // 2, lax.rem(t, 2), f // 4, lax.rem(f, 4), t


def move(value, to):
    pairs = []
    for s in range(32):
        for f in range(8):
            here = dict(z=s // 4, yl=(s // 2) % 2, c=s % 2, yh=f // 4, x=f % 4)
            change = to(**here)
            if change is None:
                continue
            there = {**here, **change}
            target = (there["z"] * 4 + there["yl"] * 2 + there["c"]) * 8 + there["yh"] * 4 + there["x"]
            pairs.append((s * 8 + f, target))
    return lax.ppermute(value, ("seq", "fsdp"), pairs)


def shape(*dims, dtype=BF16):
    return jax.ShapeDtypeStruct(dims, dtype)


def call(kernel, name, outs, ins, operands, scratch=(), mb=48, flops=0, bytes_accessed=0, out_specs=None):
    return pl.pallas_call(
        kernel,
        out_shape=outs,
        in_specs=ins,
        out_specs=jax.tree.map(lambda _: VMEM, outs) if out_specs is None else out_specs,
        scratch_shapes=scratch,
        name=name,
        compiler_params=pltpu.CompilerParams(vmem_limit_bytes=mb << 20),
        cost_estimate=pl.CostEstimate(flops=flops, bytes_accessed=bytes_accessed, transcendentals=0),
    )(*operands)


def iota2(dims, dim):
    return lax.broadcasted_iota(jnp.int32, dims, dim)


def ones_at(where):
    return jnp.where(where, 1.0, 0.0)


def anti_identity():
    return ones_at(iota2((128, 128), 0) + iota2((128, 128), 1) == 127).astype(BF16)


def flipped(block):
    anti = anti_identity()
    rows = jnp.dot(anti, block, preferred_element_type=F32).astype(BF16)
    parts = [
        jnp.dot(rows[:, 128 * j : 128 * j + 128], anti, preferred_element_type=F32).astype(BF16)
        for j in range(D // 128)
    ]
    return jnp.concatenate(parts[::-1], axis=1)


def head_pick():
    _, _, _, _, _, t = place()
    row, col = iota2((512, 128), 0), iota2((512, 128), 1)
    return ones_at(row == 256 * (col // 64) + 64 * t + lax.rem(col, 64))


def start_kernel(hidden, tokens, base_bias, iw, ow, act, ua, ub, ua_other, ub_other, rows_in, ids_in, bias_in, iw_in, ow_in, sem):
    _, yl, c, _, _, t = place()
    copies = [
        pltpu.make_async_copy(tokens, ids_in, sem.at[0]),
        pltpu.make_async_copy(base_bias, bias_in, sem.at[1]),
        pltpu.make_async_copy(hidden, rows_in, sem.at[2]),
        pltpu.make_async_copy(iw.at[pl.ds(E, WIDE - E)], iw_in.at[pl.ds(E, WIDE - E)], sem.at[3]),
        pltpu.make_async_copy(iw.at[pl.ds(0, E)], iw_in.at[pl.ds(0, E)], sem.at[4]),
        pltpu.make_async_copy(ow, ow_in, sem.at[5]),
    ]
    for copy in copies:
        copy.start()
    for copy in copies[:3]:
        copy.wait()
    ids = ids_in[...]
    letter = iota2((5, ROWS), 0)
    paired = jnp.where(ids == 4, 4, 3 - ids)
    for strand, chosen in ((0, ids), (1, paired)):
        onehot = ones_at(letter == chosen).astype(BF16)
        bias = lax.dot_general(
            onehot, bias_in[:, D * strand : D * strand + D], (((0,), (0,)), ((), ())), preferred_element_type=F32
        )
        block = (rows_in[:, D * strand : D * strand + D].astype(F32) + bias).astype(BF16)
        if strand:
            block = flipped(block)
        act[ROWS * strand : ROWS * strand + ROWS, :] = block
    for copy in copies[3:]:
        copy.wait()
    for early, late, which in ((ua, ub, t), (ua_other, ub_other, (1 - yl) * 2 + c)):
        for j in range(MINE):
            row = pl.multiple_of(256 * j + 64 * which, 64)
            early[64 * j : 64 * j + 64, :] = iw_in[pl.ds(E + row, 64), :]
            late[64 * j : 64 * j + 64, :] = iw_in[pl.ds(row, 64), :]
            out_rows = ow_in[pl.ds(pl.multiple_of(64 * which, 64), 64), 128 * j : 128 * j + 128]
            late[OWN + 64 * j : OWN + 64 * j + 64, :] = out_rows
        early[OWN : OWN + STATE, :] = iw_in[pl.ds(pl.multiple_of(2 * E + STATE * c, STATE), STATE), :]
        early[OWN + STATE :, :] = iw_in[2 * E + 2 * STATE :, :]


def hold(value, far, prm, out):
    out[...] = value[...]


def choose_halo(act, act_y, far, halo, far_out):
    _, yl, c, _, _, _ = place()
    forward = jnp.where(yl == 1, act[ROWS - HALO : ROWS, :], act_y[ROWS - HALO : ROWS, :])
    reverse = jnp.where(yl == 0, act[2 * ROWS - HALO :, :], act_y[2 * ROWS - HALO :, :])
    halo[...] = jnp.where(c == 1, forward, reverse)
    far_out[...] = far[...]


def pack_params(cw, cb, dtb, rate, gain, prm, heads, stack):
    _, _, _, _, _, t = place()
    pick = head_pick()
    stack[...] = jnp.zeros_like(stack)
    stack[0:4, :] = cw[:, :E]
    stack[4:5, :] = cb[:, :E]
    stack[5:6, :] = gain[...]
    prm[...] = jnp.zeros_like(prm)
    for j in range(4):
        prm[:, 128 * j : 128 * j + 128] = jnp.dot(
            stack[:, 512 * j : 512 * j + 512], pick, precision=EXACT, preferred_element_type=F32
        )
    prm[0:4, OWN:] = cw[:, E:]
    prm[4:5, OWN:] = cb[:, E:]
    chosen = iota2((MINE, HEADS), 1) == 4 * iota2((MINE, HEADS), 0) + t
    for n, ref in enumerate((dtb, rate)):
        column = jnp.sum(jnp.where(chosen, ref[...], 0.0), axis=1, keepdims=True)
        heads[n] = jnp.broadcast_to(column, (MINE, 128))


def pack_core(*refs):
    act, act_y, halo, ub, ub_far = refs[:5]
    units, out, late = refs[5:13], refs[13], refs[14]
    late[:LATE, :] = ub[...]
    late[LATE:, :] = ub_far[...]
    out[: 2 * ROWS, :] = act[...]
    out[2 * ROWS : 4 * ROWS, :] = act_y[...]
    out[4 * ROWS : 4 * ROWS + HALO, :] = halo[...]
    for n, unit in enumerate(units):
        out[4 * ROWS + HALO :, 128 * n : 128 * n + 128] = unit[OWN : OWN + STATE, :]


def weight_rows():
    _, _, _, yh, x, _ = place()
    return [which * 4 + lax.rem(x - k + 4, 4) for which in (yh, 1 - yh) for k in range(4)]


def place_act(act, blocks):
    _, _, _, _, _, t = place()
    for (ref, first), other in zip(blocks, (0, 2, 1, 3)):
        at = t ^ other
        for strand, row in ((0, at), (1, 3 - at)):
            act[strand, pl.ds(pl.multiple_of(HALO + ROWS * row, 16), ROWS), :] = ref[
                first + ROWS * strand : first + ROWS * strand + ROWS, :
            ]


def spread_heads(count):
    return ones_at(lax.rem(iota2((MINE * count, OWN), 0), MINE) == iota2((MINE * count, OWN), 1) // HEADDIM)


def hi_lo(v):
    hi = v.astype(BF16).astype(F32)
    return hi, v - hi


def spread_columns(rows):
    both = jnp.concatenate(hi_lo(rows), axis=0).astype(BF16)
    return lax.dot_general(
        both, spread_heads(2).astype(BF16), (((0,), (0,)), ((), ())), preferred_element_type=F32
    )


def spread_row(column):
    return jnp.sum(spread_heads(1) * column, axis=0, keepdims=True)


def running_sum(rows):
    count = rows.shape[0]
    hi, rest = hi_lo(rows)
    mid, low = hi_lo(rest)
    upper = ones_at(iota2((GROUP, GROUP), 0) <= iota2((GROUP, GROUP), 1)).astype(BF16)
    pieces = jnp.concatenate([hi, mid, low], axis=0).astype(BF16)
    sums = jnp.dot(pieces, upper, preferred_element_type=F32)
    return sums[:count] + sums[count : 2 * count] + sums[2 * count :]


def times_turned(a, b):
    return lax.dot_general(a, b, (((1,), (1,)), ((), ())), preferred_element_type=F32)


def scan_strand(strand, act, weight, prm, heads, xs, maps, sizes, sums, starts, end, proj):
    _, _, _, _, _, t = place()
    choose = ones_at(iota2((MINE, HEADS), 1) == 4 * iota2((MINE, HEADS), 0) + t).astype(BF16)
    proj[...] = times_turned(act[strand], weight[...]).astype(BF16).astype(F32)
    turned = []
    for g in range(GROUPS):
        steps = proj[HALO + GROUP * g : HALO + GROUP * g + GROUP, CONVED:].T[:HEADS].astype(BF16)
        turned.append(jnp.dot(choose, steps, preferred_element_type=F32))
    raw = jnp.concatenate(turned, axis=0) + jnp.concatenate([heads[0]] * GROUPS, axis=0)
    size = jnp.maximum(raw, 0.0) + jnp.log1p(jnp.exp(-jnp.abs(raw)))
    decay = -size * jnp.concatenate([heads[1]] * GROUPS, axis=0)
    cumulated = running_sum(decay)
    sizes[...] = size
    sums[...] = cumulated
    state = jnp.zeros((STATE, OWN), F32)
    total = jnp.zeros((MINE, 1), F32)
    for g in range(GROUPS):
        rows = slice(GROUP * g, GROUP * g + GROUP)
        for j in range(6):
            cols = slice(128 * j, 128 * j + 128)
            first = HALO - 3 + GROUP * g
            acc = prm[4:5, cols] + prm[0:1, cols] * proj[first : first + GROUP, cols]
            for k in range(1, CONV):
                acc = acc + prm[k : k + 1, cols] * proj[first + k : first + k + GROUP, cols]
            half = 0.5 * acc
            done = (half + half * jnp.tanh(half)).astype(BF16)
            if j < 4:
                xs[rows, cols] = done
            else:
                maps[rows, 128 * (j - 4) : 128 * (j - 4) + 128] = done
        part = slice(MINE * g, MINE * g + MINE)
        last = cumulated[part, GROUP - 1 :]
        total = total + last
        remaining = spread_columns(jnp.exp(last - cumulated[part]) * size[part])
        weighted = (xs[rows, :].astype(F32) * remaining).astype(BF16)
        starts[g] = state.astype(BF16)
        added = lax.dot_general(
            maps[rows, :STATE], weighted, (((0,), (0,)), ((), ())), preferred_element_type=F32
        )
        state = state * spread_row(jnp.exp(last)) + added
    end[:STATE, :] = state.astype(BF16)
    hi, lo = hi_lo(spread_row(total))
    line = iota2((HALO, OWN), 0)
    end[STATE:, :] = jnp.where(line == 0, hi, jnp.where(line == 1, lo, 0.0)).astype(BF16)


def first_scan(*refs):
    act_own, act_y, halo, swapped = refs[:4]
    units, refs = refs[4:12], refs[12:]
    prm, heads, xs, maps, sizes, sums, starts, act, weight, end, proj = refs
    z, _, c, _, _, _ = place()
    weight[CONVED + HEADS :, :] = jnp.zeros((WA - CONVED - HEADS, D), BF16)
    for n, (unit, f) in enumerate(zip(units, weight_rows())):
        lanes = pl.ds(pl.multiple_of(128 * f, 128), 128)
        weight[:OWN, lanes] = unit[:OWN, :]
        weight[pl.ds(pl.multiple_of(OWN + STATE * c, STATE), STATE), lanes] = unit[OWN : OWN + STATE, :]
        weight[pl.ds(pl.multiple_of(OWN + STATE * (1 - c), STATE), STATE), lanes] = swapped[
            4 * ROWS + HALO :, 128 * n : 128 * n + 128
        ]
        weight[CONVED : CONVED + HEADS, lanes] = unit[OWN + STATE :, :]
    place_act(act, ((act_own, 0), (act_y, 0), (swapped, 0), (swapped, 2 * ROWS)))
    near = halo[...]
    far = swapped[4 * ROWS : 4 * ROWS + HALO, :]
    act[0, :HALO, :] = jnp.where(c == 1, near, far)
    act[1, :HALO, :] = jnp.where(c == 1, far, near)
    scan_strand(1 - chain(z), act, weight, prm, heads, xs, maps, sizes, sums, starts, end, proj)


def second_scan(act, weight, prm, heads, xs, maps, sizes, sums, starts, end, proj):
    z, _, _, _, _, _ = place()
    scan_strand(chain(z), act, weight, prm, heads, xs, maps, sizes, sums, starts, end, proj)


def chain(z):
    return 1 - lax.rem(z, 2)


def decay_of(ref):
    rows = ref[STATE:, :].astype(F32)
    return rows[0:1] + rows[1:2]


def pair_state(kept, mate, out):
    decay = decay_of(kept)
    out[:STATE, :] = (kept[:STATE, :].astype(F32) + jnp.exp(decay) * mate[:STATE, :].astype(F32)).astype(BF16)
    hi, lo = hi_lo(decay + decay_of(mate))
    line = iota2((HALO, OWN), 0)
    out[STATE:, :] = jnp.where(line == 0, hi, jnp.where(line == 1, lo, 0.0)).astype(BF16)


def again(value, out):
    out[...] = value[...]


def earlier_pairs(*refs):
    *pairs, out = refs
    total = jnp.zeros((STATE, OWN), F32)
    gone = jnp.zeros((1, OWN), F32)
    for pair in pairs:
        total = total + jnp.exp(gone) * pair[:STATE, :].astype(F32)
        gone = gone + decay_of(pair)
    out[...] = total.astype(BF16)


def local_kernel(*refs):
    scans, refs = (refs[:5], refs[5:10]), refs[11:]
    local, carry, out_maps = refs
    z, _, _, _, _, _ = place()
    causal = ones_at(iota2((GROUP, GROUP), 0) >= iota2((GROUP, GROUP), 1))
    left = iota2((GROUP, 128), 1) < HEADDIM
    for strand, (xs, maps, sizes, sums, starts) in zip((1 - chain(z), chain(z)), scans):
        out_maps[strand] = maps[:, STATE:]

        def one_group(g, before, strand=strand, xs=xs, maps=maps, sizes=sizes, sums=sums, starts=starts):
            rows = pl.ds(pl.multiple_of(GROUP * g, GROUP), GROUP)
            part = pl.ds(pl.multiple_of(MINE * g, MINE), MINE)
            size = sizes[part, :]
            cumulated = sums[part, :]
            columns = jnp.concatenate([cumulated, jnp.zeros((GROUP - MINE, GROUP), F32)], axis=0).T
            in_map = maps[rows, :STATE]
            out_map = maps[rows, STATE:]
            affinity = times_turned(out_map, in_map) * causal
            parts = []
            for pair in range(4):
                mixes = []
                for h in (2 * pair, 2 * pair + 1):
                    gap = jnp.minimum(columns[:, h : h + 1] - cumulated[h : h + 1, :], 0.0)
                    mixes.append((affinity * jnp.exp(gap) * size[h : h + 1, :]).astype(BF16))
                x = xs[rows, 128 * pair : 128 * pair + 128]
                zero = jnp.zeros_like(x)
                tall = jnp.concatenate([jnp.where(left, x, zero), jnp.where(left, zero, x)], axis=0)
                parts.append(jnp.dot(jnp.concatenate(mixes, axis=1), tall, preferred_element_type=F32))
            within = jnp.concatenate(parts, axis=1)
            grown = spread_columns(jnp.exp(cumulated))
            local[strand, rows, :] = within + jnp.dot(out_map, starts[g], preferred_element_type=F32) * grown
            carry[strand, rows, :] = grown * spread_row(jnp.exp(before))
            return before + cumulated[:, GROUP - 1 :]

        lax.fori_loop(0, GROUPS, one_group, jnp.zeros((MINE, 1), F32))


def gate_kernel(act, *refs):
    received, refs = refs[:4], refs[4:]
    gate, out_weight, weight = refs
    _, _, _, yh, x, _ = place()
    units = []
    for k, unit in enumerate(received):
        for n, which in enumerate((yh, 1 - yh)):
            units.append((unit, LATE * n, which * 4 + lax.rem(x - k + 4, 4)))
    for unit, first, f in units:
        lanes = pl.ds(pl.multiple_of(128 * f, 128), 128)
        weight[:, lanes] = unit[first : first + OWN, :]
        rows = pl.ds(pl.multiple_of(64 * f, 64), 64)
        for j in range(8):
            line = first + OWN + 64 * j
            out_weight[j // 4, rows, 128 * (j % 4) : 128 * (j % 4) + 128] = unit[line : line + 64, :]
    for strand in range(2):
        half = 0.5 * times_turned(act[strand, HALO:, :], weight[...]).astype(BF16).astype(F32)
        gate[strand] = half + half * jnp.tanh(half)


def half_rows(own):
    _, yl, _, _, _, _ = place()
    y = yl if own else 1 - yl
    return 256 * y, 256 * (1 - y)


def project_half(own, weight, entering, prm, maps, local, carry, gate, keep, give, normed):
    _, _, c, _, _, _ = place()
    gain = prm[5:6, :OWN]
    tails = []
    for strand, first in enumerate(half_rows(own)):
        for b in range(2):
            rows = pl.ds(pl.multiple_of(first + ROWS * b, ROWS), ROWS)
            held = jnp.dot(maps[strand, rows, :], entering[strand], preferred_element_type=F32)
            gated = (local[strand, rows, :] + held * carry[strand, rows, :]) * gate[strand, rows, :]
            squared = gated * gated
            folded = (squared[:, :128] + squared[:, 128:256]) + (squared[:, 256:384] + squared[:, 384:])
            tails.append(jnp.sum(folded.T, axis=0, keepdims=True))
            normed[2 * strand + b] = (gated * gain).astype(BF16)
    line = iota2((HALO, ROWS), 0)
    for ref, core in ((keep, c), (give, 1 - c)):
        for strand in range(2):
            b = core if strand == 0 else 1 - core
            for half in range(2):
                ref[ROWS * strand : ROWS * strand + ROWS, 512 * half : 512 * half + 512] = jnp.dot(
                    normed[2 * strand + b], weight[half], preferred_element_type=F32
                ).astype(BF16)
            hi, lo = hi_lo(jnp.where(b == 0, tails[2 * strand], tails[2 * strand + 1]))
            tail = jnp.where(line == 0, hi, jnp.where(line == 1, lo, 0.0))
            ref[2 * ROWS :, ROWS * strand : ROWS * strand + ROWS] = tail.astype(BF16)
        ref[2 * ROWS :, 2 * ROWS :] = jnp.zeros((HALO, D - 2 * ROWS), BF16)


def first_half(*refs):
    mate, entered, mate_entered, refs = refs[0], refs[1], refs[2], refs[3:]
    weight, prm, maps, local, carry, gate, entering, keep, give, normed = refs
    z, _, _, _, _, _ = place()
    role = chain(z)
    entering[role] = (
        mate[:STATE, :].astype(F32) + jnp.exp(decay_of(mate)) * entered[...].astype(F32)
    ).astype(BF16)
    entering[1 - role] = mate_entered[...]
    project_half(False, weight, entering, prm, maps, local, carry, gate, keep, give, normed)


def second_half(weight, entering, prm, maps, local, carry, gate, keep, give, normed):
    project_half(True, weight, entering, prm, maps, local, carry, gate, keep, give, normed)


def pair_sum(mine, came, second, out):
    main = mine[: 2 * ROWS, :].astype(F32) + came[: 2 * ROWS, :].astype(F32)
    out[: 2 * ROWS, :] = main.astype(BF16)
    tail = mine[2 * ROWS :, :].astype(F32) + came[2 * ROWS :, :].astype(F32)
    hi, lo = hi_lo(tail[0:1] + tail[1:2])
    line = iota2((HALO, D), 0)
    out[2 * ROWS :, :] = jnp.where(line == 0, hi, jnp.where(line == 1, lo, 0.0)).astype(BF16)


def last_kernel(mine, came, far, out):
    def tail(ref):
        rows = ref[2 * ROWS :, :].astype(F32)
        return rows[0:1] + rows[1:2]

    squares = tail(mine) + tail(came) + tail(far)
    diagonal = iota2((ROWS, ROWS), 0) == iota2((ROWS, ROWS), 1)
    for strand in range(2):
        rows = slice(ROWS * strand, ROWS * strand + ROWS)
        mean = jnp.sum(jnp.where(diagonal, squares[:, rows], 0.0), axis=1, keepdims=True) * (1.0 / E)
        main = mine[rows, :].astype(F32) + came[rows, :].astype(F32) + far[rows, :].astype(F32)
        block = (main * lax.rsqrt(mean + 1e-05)).astype(BF16)
        if strand:
            block = flipped(block)
        out[:, D * strand : D * strand + D] = block


def swap_core(value):
    return move(value, lambda z, yl, c, yh, x: dict(c=1 - c))


def swap_y(value):
    return move(value, lambda z, yl, c, yh, x: dict(yl=1 - yl))


def swap_diagonal(value, k=0):
    return move(value, lambda z, yl, c, yh, x: dict(yl=1 - yl, yh=1 - yh, x=(x + k) % 4))


def along_x(value, k):
    return move(value, lambda z, yl, c, yh, x: dict(x=(x + k) % 4))


def pair_step(m):
    def to(z, yl, c, yh, x):
        target = z + 2 * m if z % 2 else z - 2 * m
        return dict(z=target) if 0 <= target < Z else None

    return to


def halo_step(z, yl, c, yh, x):
    target = z + 1 if c else z - 1
    return dict(z=target) if 0 <= target < Z else None


def body(hidden, tokens, base_bias, in_weight, conv_weight, conv_bias, dt_bias, decay_rate, norm_gain, out_weight):
    act, ua, ub, ua_other, ub_other = call(
        start_kernel,
        "start_kernel",
        [shape(2 * ROWS, D)] + [shape(UNIT, 128), shape(LATE, 128)] * 2,
        [ANY] * 5,
        tuple(
            pltpu.with_memory_space_constraint(value, pltpu.HBM)
            for value in (hidden[0], tokens, base_bias, in_weight.T, out_weight)
        ),
        scratch=[
            pltpu.VMEM((ROWS, 2 * D), BF16),
            pltpu.VMEM((1, ROWS), jnp.int32),
            pltpu.VMEM((5, 2 * D), BF16),
            pltpu.VMEM((WIDE, ROWS), BF16),
            pltpu.VMEM((2 * ROWS, D), BF16),
            pltpu.SemaphoreType.DMA((6,)),
        ],
        mb=16,
    )
    act_y = swap_y(act)
    far = swap_diagonal(ua_other)
    own_1, own_3, own_2 = along_x(ua, 1), along_x(ua, 3), along_x(ua, 2)
    prm, heads = call(
        pack_params,
        "pack_params",
        [shape(8, CONVED, dtype=F32), shape(2, MINE, 128, dtype=F32)],
        [VMEM] * 5,
        (conv_weight, conv_bias[None], dt_bias[None], decay_rate[None], norm_gain[None]),
        scratch=[pltpu.VMEM((8, E), F32)],
        mb=12,
    )
    ub_other = call(hold, "hold", shape(LATE, 128), [VMEM] * 3, (ub_other, far, prm), mb=8)
    far_1, far_3 = along_x(far, 1), along_x(far, 3)
    ub_far = swap_diagonal(ub_other)
    halo, far_late = call(
        choose_halo, "choose_halo", [shape(HALO, D), shape(UNIT, 128)], [VMEM] * 3, (act, act_y, far), mb=8
    )
    halo = move(halo, halo_step)
    far_2 = along_x(far_late, 2)
    units = (ua, own_1, own_2, own_3, far, far_1, far_2, far_3)
    payload, late = call(
        pack_core,
        "pack_core",
        [shape(PAYLOAD, D), shape(2 * LATE, 128)],
        [VMEM] * 13,
        (act, act_y, halo, ub, ub_far, *units),
        mb=12,
    )
    swapped = swap_core(payload)
    late = (late, *[along_x(late, k) for k in (1, 2, 3)])
    scanned = [
        shape(SPAN, OWN),
        shape(SPAN, 2 * STATE),
        shape(MINE * GROUPS, GROUP, dtype=F32),
        shape(MINE * GROUPS, GROUP, dtype=F32),
        shape(GROUPS, STATE, OWN),
    ]
    *first, act, weight, given = call(
        first_scan,
        "first_scan",
        scanned + [shape(2, PAD, D), shape(WA, D), shape(STATE + HALO, OWN)],
        [VMEM] * 14,
        (act, act_y, halo, swapped, *units, prm, heads),
        scratch=[pltpu.VMEM((PAD, WA), F32)],
        mb=20,
        flops=1056 * D * WA,
        bytes_accessed=8 << 20,
    )
    *second, kept = call(
        second_scan,
        "second_scan",
        scanned + [shape(STATE + HALO, OWN)],
        [VMEM] * 4,
        (act, weight, prm, heads),
        scratch=[pltpu.VMEM((PAD, WA), F32)],
        mb=20,
        flops=16896 * D * WA,
        bytes_accessed=8 << 20,
    )
    mate = move(given, lambda z, yl, c, yh, x: dict(z=z ^ 1))
    pair = call(pair_state, "pair_state", shape(STATE + HALO, OWN), [VMEM] * 2, (kept, mate), mb=8)
    far_first = []
    for m in (3, 2, 1):
        far_first.append(move(pair, pair_step(m)))
        if m > 1:
            pair = call(again, "again", shape(STATE + HALO, OWN), [VMEM], (pair,), mb=8)
    earlier = far_first[::-1]
    local, carry, maps = call(
        local_kernel,
        "local_kernel",
        [shape(2, SPAN, OWN, dtype=F32)] * 2 + [shape(2, SPAN, STATE)],
        [VMEM] * 11,
        (*first, *second, pair),
        mb=16,
        flops=8 * 1024 * D * OWN,
        bytes_accessed=16 << 20,
    )
    entered = call(earlier_pairs, "earlier_pairs", shape(STATE, OWN), [VMEM] * 3, earlier, mb=8)
    mate_entered = move(entered, lambda z, yl, c, yh, x: dict(z=z ^ 1))
    gate, weight = call(
        gate_kernel,
        "gate_kernel",
        [shape(2, SPAN, OWN, dtype=F32), shape(2, OWN, 512)],
        [VMEM] * (1 + len(late)),
        (act, *late),
        scratch=[pltpu.VMEM((OWN, D), BF16)],
        mb=16,
        flops=2 * 1024 * D * OWN,
        bytes_accessed=8 << 20,
    )
    half_out = [shape(2 * ROWS + HALO, D)] * 2
    half_scratch = [pltpu.VMEM((4, ROWS, OWN), BF16)]
    entering, keep, give = call(
        first_half,
        "first_half",
        [shape(2, STATE, OWN)] + half_out,
        [VMEM] * 9,
        (mate, entered, mate_entered, weight, prm, maps, local, carry, gate),
        scratch=half_scratch,
        mb=16,
        flops=1024 * D * OWN,
        bytes_accessed=4 << 20,
    )
    keep_2, give_2 = call(
        second_half,
        "second_half",
        half_out,
        [VMEM] * 7,
        (weight, entering, prm, maps, local, carry, gate),
        scratch=half_scratch,
        mb=16,
        flops=1024 * D * OWN,
        bytes_accessed=4 << 20,
    )
    part = call(
        pair_sum, "pair_sum", shape(2 * ROWS + HALO, D), [VMEM] * 3, (keep, swap_core(give), keep_2), mb=8
    )
    far_part = swap_y(part)
    out = call(last_kernel, "last_kernel", shape(ROWS, 2 * D), [VMEM] * 3, (keep_2, swap_core(give_2), far_part), mb=8)
    return out[None]


def solution(mesh):
    placed = (
        P("fsdp", "seq", None),
        P("fsdp", "seq"),
        P(),
        P("fsdp", None),
        P(),
        P(),
        P(),
        P(),
        P(),
        P("fsdp", None),
    )
    return jax.shard_map(
        body, mesh=mesh, in_specs=placed, out_specs=P("fsdp", "seq", None), check_vma=False
    )
```

```python
import jax
import jax.numpy as jnp
from jax import lax
from jax.experimental import pallas as pl
from jax.experimental.pallas import tpu as pltpu
from jax.sharding import PartitionSpec as P

D = 1024
HEADS = 32
HEADDIM = 64
STATE = 128
CONV = 4
GROUP = 128
E = 2048
WIDE = 4384
ROWS = 128
SPAN = 512
GROUPS = SPAN // GROUP
OWN = 512
MINE = 8
HALO = 16
PAD = HALO + SPAN
CONVED = OWN + 2 * STATE
WA = CONVED + 128
UNIT = OWN + STATE + HEADS
LATE = 2 * OWN
Z = 8
PAYLOAD = 4 * ROWS + HALO + STATE

F32 = jnp.float32
BF16 = jnp.bfloat16
EXACT = lax.Precision.HIGHEST
ANY = pl.BlockSpec(memory_space=pl.ANY)
VMEM = pl.BlockSpec(memory_space=pltpu.VMEM)


def place():
    s, f = lax.axis_index("seq"), lax.axis_index("fsdp")
    t = lax.rem(s, 4)
    return s // 4, t // 2, lax.rem(t, 2), f // 4, lax.rem(f, 4), t


def move(value, to):
    pairs = []
    for s in range(32):
        for f in range(8):
            here = dict(z=s // 4, yl=(s // 2) % 2, c=s % 2, yh=f // 4, x=f % 4)
            change = to(**here)
            if change is None:
                continue
            there = {**here, **change}
            target = (there["z"] * 4 + there["yl"] * 2 + there["c"]) * 8 + there["yh"] * 4 + there["x"]
            pairs.append((s * 8 + f, target))
    return lax.ppermute(value, ("seq", "fsdp"), pairs)


def shape(*dims, dtype=BF16):
    return jax.ShapeDtypeStruct(dims, dtype)


def call(kernel, name, outs, ins, operands, scratch=(), mb=48, flops=0, bytes_accessed=0, out_specs=None):
    return pl.pallas_call(
        kernel,
        out_shape=outs,
        in_specs=ins,
        out_specs=jax.tree.map(lambda _: VMEM, outs) if out_specs is None else out_specs,
        scratch_shapes=scratch,
        name=name,
        compiler_params=pltpu.CompilerParams(vmem_limit_bytes=mb << 20),
        cost_estimate=pl.CostEstimate(flops=flops, bytes_accessed=bytes_accessed, transcendentals=0),
    )(*operands)


def iota2(dims, dim):
    return lax.broadcasted_iota(jnp.int32, dims, dim)


def ones_at(where):
    return jnp.where(where, 1.0, 0.0)


def anti_identity():
    return ones_at(iota2((128, 128), 0) + iota2((128, 128), 1) == 127).astype(BF16)


def flipped(block):
    anti = anti_identity()
    rows = jnp.dot(anti, block, preferred_element_type=F32).astype(BF16)
    parts = [
        jnp.dot(rows[:, 128 * j : 128 * j + 128], anti, preferred_element_type=F32).astype(BF16)
        for j in range(D // 128)
    ]
    return jnp.concatenate(parts[::-1], axis=1)


def head_pick():
    _, _, _, _, _, t = place()
    row, col = iota2((512, 128), 0), iota2((512, 128), 1)
    return ones_at(row == 256 * (col // 64) + 64 * t + lax.rem(col, 64))


def start_kernel(hidden, tokens, base_bias, iw, ow, act, ua, ub, ua_other, ub_other, rows_in, ids_in, bias_in, iw_in, ow_in, sem):
    _, yl, c, _, _, t = place()
    copies = [
        pltpu.make_async_copy(tokens, ids_in, sem.at[0]),
        pltpu.make_async_copy(base_bias, bias_in, sem.at[1]),
        pltpu.make_async_copy(hidden, rows_in, sem.at[2]),
        pltpu.make_async_copy(iw.at[pl.ds(E, WIDE - E)], iw_in.at[pl.ds(E, WIDE - E)], sem.at[3]),
        pltpu.make_async_copy(iw.at[pl.ds(0, E)], iw_in.at[pl.ds(0, E)], sem.at[4]),
        pltpu.make_async_copy(ow, ow_in, sem.at[5]),
    ]
    for copy in copies:
        copy.start()
    for copy in copies[:3]:
        copy.wait()
    ids = ids_in[...]
    letter = iota2((5, ROWS), 0)
    paired = jnp.where(ids == 4, 4, 3 - ids)
    for strand, chosen in ((0, ids), (1, paired)):
        onehot = ones_at(letter == chosen).astype(BF16)
        bias = lax.dot_general(
            onehot, bias_in[:, D * strand : D * strand + D], (((0,), (0,)), ((), ())), preferred_element_type=F32
        )
        block = (rows_in[:, D * strand : D * strand + D].astype(F32) + bias).astype(BF16)
        if strand:
            block = flipped(block)
        act[ROWS * strand : ROWS * strand + ROWS, :] = block
    for copy in copies[3:]:
        copy.wait()
    for early, late, which in ((ua, ub, t), (ua_other, ub_other, (1 - yl) * 2 + c)):
        for j in range(MINE):
            row = pl.multiple_of(256 * j + 64 * which, 64)
            early[64 * j : 64 * j + 64, :] = iw_in[pl.ds(E + row, 64), :]
            late[64 * j : 64 * j + 64, :] = iw_in[pl.ds(row, 64), :]
            out_rows = ow_in[pl.ds(pl.multiple_of(64 * which, 64), 64), 128 * j : 128 * j + 128]
            late[OWN + 64 * j : OWN + 64 * j + 64, :] = out_rows
        early[OWN : OWN + STATE, :] = iw_in[pl.ds(pl.multiple_of(2 * E + STATE * c, STATE), STATE), :]
        early[OWN + STATE :, :] = iw_in[2 * E + 2 * STATE :, :]


def hold(value, far, prm, out):
    out[...] = value[...]


def choose_halo(act, act_y, far, halo, far_out):
    _, yl, c, _, _, _ = place()
    forward = jnp.where(yl == 1, act[ROWS - HALO : ROWS, :], act_y[ROWS - HALO : ROWS, :])
    reverse = jnp.where(yl == 0, act[2 * ROWS - HALO :, :], act_y[2 * ROWS - HALO :, :])
    halo[...] = jnp.where(c == 1, forward, reverse)
    far_out[...] = far[...]


def pack_params(cw, cb, dtb, rate, gain, prm, heads, stack):
    _, _, _, _, _, t = place()
    pick = head_pick()
    stack[...] = jnp.zeros_like(stack)
    stack[0:4, :] = cw[:, :E]
    stack[4:5, :] = cb[:, :E]
    stack[5:6, :] = gain[...]
    prm[...] = jnp.zeros_like(prm)
    for j in range(4):
        prm[:, 128 * j : 128 * j + 128] = jnp.dot(
            stack[:, 512 * j : 512 * j + 512], pick, precision=EXACT, preferred_element_type=F32
        )
    prm[0:4, OWN:] = cw[:, E:]
    prm[4:5, OWN:] = cb[:, E:]
    chosen = iota2((MINE, HEADS), 1) == 4 * iota2((MINE, HEADS), 0) + t
    for n, ref in enumerate((dtb, rate)):
        column = jnp.sum(jnp.where(chosen, ref[...], 0.0), axis=1, keepdims=True)
        heads[n] = jnp.broadcast_to(column, (MINE, 128))


def pack_core(*refs):
    act, act_y, halo, ub, ub_far = refs[:5]
    units, out, late = refs[5:13], refs[13], refs[14]
    late[:LATE, :] = ub[...]
    late[LATE:, :] = ub_far[...]
    out[: 2 * ROWS, :] = act[...]
    out[2 * ROWS : 4 * ROWS, :] = act_y[...]
    out[4 * ROWS : 4 * ROWS + HALO, :] = halo[...]
    for n, unit in enumerate(units):
        out[4 * ROWS + HALO :, 128 * n : 128 * n + 128] = unit[OWN : OWN + STATE, :]


def weight_rows():
    _, _, _, yh, x, _ = place()
    return [which * 4 + lax.rem(x - k + 4, 4) for which in (yh, 1 - yh) for k in range(4)]


def place_act(act, blocks):
    _, _, _, _, _, t = place()
    for (ref, first), other in zip(blocks, (0, 2, 1, 3)):
        at = t ^ other
        for strand, row in ((0, at), (1, 3 - at)):
            act[strand, pl.ds(pl.multiple_of(HALO + ROWS * row, 16), ROWS), :] = ref[
                first + ROWS * strand : first + ROWS * strand + ROWS, :
            ]


def spread_heads(count):
    return ones_at(lax.rem(iota2((MINE * count, OWN), 0), MINE) == iota2((MINE * count, OWN), 1) // HEADDIM)


def hi_lo(v):
    hi = v.astype(BF16).astype(F32)
    return hi, v - hi


def spread_columns(rows):
    both = jnp.concatenate(hi_lo(rows), axis=0).astype(BF16)
    return lax.dot_general(
        both, spread_heads(2).astype(BF16), (((0,), (0,)), ((), ())), preferred_element_type=F32
    )


def spread_row(column):
    return jnp.sum(spread_heads(1) * column, axis=0, keepdims=True)


def running_sum(rows):
    count = rows.shape[0]
    hi, rest = hi_lo(rows)
    mid, low = hi_lo(rest)
    upper = ones_at(iota2((GROUP, GROUP), 0) <= iota2((GROUP, GROUP), 1)).astype(BF16)
    pieces = jnp.concatenate([hi, mid, low], axis=0).astype(BF16)
    sums = jnp.dot(pieces, upper, preferred_element_type=F32)
    return sums[:count] + sums[count : 2 * count] + sums[2 * count :]


def times_turned(a, b):
    return lax.dot_general(a, b, (((1,), (1,)), ((), ())), preferred_element_type=F32)


def scan_strand(strand, act, weight, prm, heads, xs, maps, sizes, sums, starts, end, proj):
    _, _, _, _, _, t = place()
    choose = ones_at(iota2((MINE, HEADS), 1) == 4 * iota2((MINE, HEADS), 0) + t).astype(BF16)
    proj[...] = times_turned(act[strand], weight[...]).astype(BF16).astype(F32)
    turned = []
    for g in range(GROUPS):
        steps = proj[HALO + GROUP * g : HALO + GROUP * g + GROUP, CONVED:].T[:HEADS].astype(BF16)
        turned.append(jnp.dot(choose, steps, preferred_element_type=F32))
    raw = jnp.concatenate(turned, axis=0) + jnp.concatenate([heads[0]] * GROUPS, axis=0)
    size = jnp.maximum(raw, 0.0) + jnp.log1p(jnp.exp(-jnp.abs(raw)))
    decay = -size * jnp.concatenate([heads[1]] * GROUPS, axis=0)
    cumulated = running_sum(decay)
    sizes[...] = size
    sums[...] = cumulated
    state = jnp.zeros((STATE, OWN), F32)
    total = jnp.zeros((MINE, 1), F32)
    for g in range(GROUPS):
        rows = slice(GROUP * g, GROUP * g + GROUP)
        for j in range(6):
            cols = slice(128 * j, 128 * j + 128)
            first = HALO - 3 + GROUP * g
            acc = prm[4:5, cols] + prm[0:1, cols] * proj[first : first + GROUP, cols]
            for k in range(1, CONV):
                acc = acc + prm[k : k + 1, cols] * proj[first + k : first + k + GROUP, cols]
            half = 0.5 * acc
            done = (half + half * jnp.tanh(half)).astype(BF16)
            if j < 4:
                xs[rows, cols] = done
            else:
                maps[rows, 128 * (j - 4) : 128 * (j - 4) + 128] = done
        part = slice(MINE * g, MINE * g + MINE)
        last = cumulated[part, GROUP - 1 :]
        total = total + last
        remaining = spread_columns(jnp.exp(last - cumulated[part]) * size[part])
        weighted = (xs[rows, :].astype(F32) * remaining).astype(BF16)
        starts[g] = state.astype(BF16)
        added = lax.dot_general(
            maps[rows, :STATE], weighted, (((0,), (0,)), ((), ())), preferred_element_type=F32
        )
        state = state * spread_row(jnp.exp(last)) + added
    end[:STATE, :] = state.astype(BF16)
    hi, lo = hi_lo(spread_row(total))
    line = iota2((HALO, OWN), 0)
    end[STATE:, :] = jnp.where(line == 0, hi, jnp.where(line == 1, lo, 0.0)).astype(BF16)


def first_scan(*refs):
    act_own, act_y, halo, swapped = refs[:4]
    units, refs = refs[4:12], refs[12:]
    prm, heads, xs, maps, sizes, sums, starts, act, weight, end, proj = refs
    z, _, c, _, _, _ = place()
    weight[CONVED + HEADS :, :] = jnp.zeros((WA - CONVED - HEADS, D), BF16)
    for n, (unit, f) in enumerate(zip(units, weight_rows())):
        lanes = pl.ds(pl.multiple_of(128 * f, 128), 128)
        weight[:OWN, lanes] = unit[:OWN, :]
        weight[pl.ds(pl.multiple_of(OWN + STATE * c, STATE), STATE), lanes] = unit[OWN : OWN + STATE, :]
        weight[pl.ds(pl.multiple_of(OWN + STATE * (1 - c), STATE), STATE), lanes] = swapped[
            4 * ROWS + HALO :, 128 * n : 128 * n + 128
        ]
        weight[CONVED : CONVED + HEADS, lanes] = unit[OWN + STATE :, :]
    place_act(act, ((act_own, 0), (act_y, 0), (swapped, 0), (swapped, 2 * ROWS)))
    near = halo[...]
    far = swapped[4 * ROWS : 4 * ROWS + HALO, :]
    act[0, :HALO, :] = jnp.where(c == 1, near, far)
    act[1, :HALO, :] = jnp.where(c == 1, far, near)
    scan_strand(1 - chain(z), act, weight, prm, heads, xs, maps, sizes, sums, starts, end, proj)


def second_scan(act, weight, prm, heads, xs, maps, sizes, sums, starts, end, proj):
    z, _, _, _, _, _ = place()
    scan_strand(chain(z), act, weight, prm, heads, xs, maps, sizes, sums, starts, end, proj)


def chain(z):
    return 1 - lax.rem(z, 2)


def decay_of(ref):
    rows = ref[STATE:, :].astype(F32)
    return rows[0:1] + rows[1:2]


def pair_state(kept, mate, out):
    decay = decay_of(kept)
    out[:STATE, :] = (kept[:STATE, :].astype(F32) + jnp.exp(decay) * mate[:STATE, :].astype(F32)).astype(BF16)
    hi, lo = hi_lo(decay + decay_of(mate))
    line = iota2((HALO, OWN), 0)
    out[STATE:, :] = jnp.where(line == 0, hi, jnp.where(line == 1, lo, 0.0)).astype(BF16)


def earlier_pairs(*refs):
    second, first, third, out = refs
    total = jnp.zeros((STATE, OWN), F32)
    gone = jnp.zeros((1, OWN), F32)
    for pair in (first, second, third):
        total = total + jnp.exp(gone) * pair[:STATE, :].astype(F32)
        gone = gone + decay_of(pair)
    out[...] = total.astype(BF16)


def local_kernel(*refs):
    scans, refs = (refs[:5], refs[5:10]), refs[11:]
    local, carry, out_maps = refs
    z, _, _, _, _, _ = place()
    causal = ones_at(iota2((GROUP, GROUP), 0) >= iota2((GROUP, GROUP), 1))
    left = iota2((GROUP, 128), 1) < HEADDIM
    for strand, (xs, maps, sizes, sums, starts) in zip((1 - chain(z), chain(z)), scans):
        out_maps[strand] = maps[:, STATE:]

        def one_group(g, before, strand=strand, xs=xs, maps=maps, sizes=sizes, sums=sums, starts=starts):
            rows = pl.ds(pl.multiple_of(GROUP * g, GROUP), GROUP)
            part = pl.ds(pl.multiple_of(MINE * g, MINE), MINE)
            size = sizes[part, :]
            cumulated = sums[part, :]
            columns = jnp.concatenate([cumulated, jnp.zeros((GROUP - MINE, GROUP), F32)], axis=0).T
            in_map = maps[rows, :STATE]
            out_map = maps[rows, STATE:]
            affinity = times_turned(out_map, in_map) * causal
            parts = []
            for pair in range(4):
                mixes = []
                for h in (2 * pair, 2 * pair + 1):
                    gap = jnp.minimum(columns[:, h : h + 1] - cumulated[h : h + 1, :], 0.0)
                    mixes.append((affinity * jnp.exp(gap) * size[h : h + 1, :]).astype(BF16))
                x = xs[rows, 128 * pair : 128 * pair + 128]
                zero = jnp.zeros_like(x)
                tall = jnp.concatenate([jnp.where(left, x, zero), jnp.where(left, zero, x)], axis=0)
                parts.append(jnp.dot(jnp.concatenate(mixes, axis=1), tall, preferred_element_type=F32))
            within = jnp.concatenate(parts, axis=1)
            grown = spread_columns(jnp.exp(cumulated))
            local[strand, rows, :] = within + jnp.dot(out_map, starts[g], preferred_element_type=F32) * grown
            carry[strand, rows, :] = grown * spread_row(jnp.exp(before))
            return before + cumulated[:, GROUP - 1 :]

        lax.fori_loop(0, GROUPS, one_group, jnp.zeros((MINE, 1), F32))


def gate_kernel(act, *refs):
    received, refs = refs[:4], refs[4:]
    gate, out_weight, weight = refs
    _, _, _, yh, x, _ = place()
    units = []
    for k, unit in enumerate(received):
        for n, which in enumerate((yh, 1 - yh)):
            units.append((unit, LATE * n, which * 4 + lax.rem(x - k + 4, 4)))
    for unit, first, f in units:
        lanes = pl.ds(pl.multiple_of(128 * f, 128), 128)
        weight[:, lanes] = unit[first : first + OWN, :]
        rows = pl.ds(pl.multiple_of(64 * f, 64), 64)
        for j in range(8):
            line = first + OWN + 64 * j
            out_weight[j // 4, rows, 128 * (j % 4) : 128 * (j % 4) + 128] = unit[line : line + 64, :]
    for strand in range(2):
        half = 0.5 * times_turned(act[strand, HALO:, :], weight[...]).astype(BF16).astype(F32)
        gate[strand] = half + half * jnp.tanh(half)


def half_rows(own):
    _, yl, _, _, _, _ = place()
    y = yl if own else 1 - yl
    return 256 * y, 256 * (1 - y)


def project_half(own, weight, entering, prm, maps, local, carry, gate, keep, give, normed):
    _, _, c, _, _, _ = place()
    gain = prm[5:6, :OWN]
    tails = []
    for strand, first in enumerate(half_rows(own)):
        for b in range(2):
            rows = pl.ds(pl.multiple_of(first + ROWS * b, ROWS), ROWS)
            held = jnp.dot(maps[strand, rows, :], entering[strand], preferred_element_type=F32)
            gated = (local[strand, rows, :] + held * carry[strand, rows, :]) * gate[strand, rows, :]
            squared = gated * gated
            folded = (squared[:, :128] + squared[:, 128:256]) + (squared[:, 256:384] + squared[:, 384:])
            tails.append(jnp.sum(folded.T, axis=0, keepdims=True))
            normed[2 * strand + b] = (gated * gain).astype(BF16)
    line = iota2((HALO, ROWS), 0)
    for ref, core in ((keep, c), (give, 1 - c)):
        for strand in range(2):
            b = core if strand == 0 else 1 - core
            for half in range(2):
                ref[ROWS * strand : ROWS * strand + ROWS, 512 * half : 512 * half + 512] = jnp.dot(
                    normed[2 * strand + b], weight[half], preferred_element_type=F32
                ).astype(BF16)
            hi, lo = hi_lo(jnp.where(b == 0, tails[2 * strand], tails[2 * strand + 1]))
            tail = jnp.where(line == 0, hi, jnp.where(line == 1, lo, 0.0))
            ref[2 * ROWS :, ROWS * strand : ROWS * strand + ROWS] = tail.astype(BF16)
        ref[2 * ROWS :, 2 * ROWS :] = jnp.zeros((HALO, D - 2 * ROWS), BF16)


def first_half(*refs):
    mate, entered, mate_entered, refs = refs[0], refs[1], refs[2], refs[3:]
    weight, prm, maps, local, carry, gate, entering, keep, give, normed = refs
    z, _, _, _, _, _ = place()
    role = chain(z)
    entering[role] = (
        mate[:STATE, :].astype(F32) + jnp.exp(decay_of(mate)) * entered[...].astype(F32)
    ).astype(BF16)
    entering[1 - role] = mate_entered[...]
    project_half(False, weight, entering, prm, maps, local, carry, gate, keep, give, normed)


def second_half(weight, entering, prm, maps, local, carry, gate, keep, give, normed):
    project_half(True, weight, entering, prm, maps, local, carry, gate, keep, give, normed)


def pair_sum(mine, came, second, out):
    main = mine[: 2 * ROWS, :].astype(F32) + came[: 2 * ROWS, :].astype(F32)
    out[: 2 * ROWS, :] = main.astype(BF16)
    tail = mine[2 * ROWS :, :].astype(F32) + came[2 * ROWS :, :].astype(F32)
    hi, lo = hi_lo(tail[0:1] + tail[1:2])
    line = iota2((HALO, D), 0)
    out[2 * ROWS :, :] = jnp.where(line == 0, hi, jnp.where(line == 1, lo, 0.0)).astype(BF16)


def last_kernel(mine, came, far, out, held, sem):
    def tail(ref):
        rows = ref[2 * ROWS :, :].astype(F32)
        return rows[0:1] + rows[1:2]

    squares = tail(mine) + tail(came) + tail(far)
    diagonal = iota2((ROWS, ROWS), 0) == iota2((ROWS, ROWS), 1)
    copies = []
    for strand in range(2):
        rows = slice(ROWS * strand, ROWS * strand + ROWS)
        mean = jnp.sum(jnp.where(diagonal, squares[:, rows], 0.0), axis=1, keepdims=True) * (1.0 / E)
        main = mine[rows, :].astype(F32) + came[rows, :].astype(F32) + far[rows, :].astype(F32)
        block = (main * lax.rsqrt(mean + 1e-05)).astype(BF16)
        if strand:
            block = flipped(block)
        held[strand] = block
        copies.append(pltpu.make_async_copy(held.at[strand], out.at[:, pl.ds(D * strand, D)], sem.at[strand]))
        copies[-1].start()
    for copy in copies:
        copy.wait()


def swap_core(value):
    return move(value, lambda z, yl, c, yh, x: dict(c=1 - c))


def swap_y(value):
    return move(value, lambda z, yl, c, yh, x: dict(yl=1 - yl))


def swap_diagonal(value, k=0):
    return move(value, lambda z, yl, c, yh, x: dict(yl=1 - yl, yh=1 - yh, x=(x + k) % 4))


def along_x(value, k):
    return move(value, lambda z, yl, c, yh, x: dict(x=(x + k) % 4))


def pair_step(m):
    def to(z, yl, c, yh, x):
        target = z + 2 * m if z % 2 else z - 2 * m
        return dict(z=target) if 0 <= target < Z else None

    return to


def halo_step(z, yl, c, yh, x):
    target = z + 1 if c else z - 1
    return dict(z=target) if 0 <= target < Z else None


def body(hidden, tokens, base_bias, in_weight, conv_weight, conv_bias, dt_bias, decay_rate, norm_gain, out_weight):
    act, ua, ub, ua_other, ub_other = call(
        start_kernel,
        "start_kernel",
        [shape(2 * ROWS, D)] + [shape(UNIT, 128), shape(LATE, 128)] * 2,
        [ANY] * 5,
        tuple(
            pltpu.with_memory_space_constraint(value, pltpu.HBM)
            for value in (hidden[0], tokens, base_bias, in_weight.T, out_weight)
        ),
        scratch=[
            pltpu.VMEM((ROWS, 2 * D), BF16),
            pltpu.VMEM((1, ROWS), jnp.int32),
            pltpu.VMEM((5, 2 * D), BF16),
            pltpu.VMEM((WIDE, ROWS), BF16),
            pltpu.VMEM((2 * ROWS, D), BF16),
            pltpu.SemaphoreType.DMA((6,)),
        ],
        mb=16,
    )
    act_y = swap_y(act)
    far = swap_diagonal(ua_other)
    own_1, own_3, own_2 = along_x(ua, 1), along_x(ua, 3), along_x(ua, 2)
    prm, heads = call(
        pack_params,
        "pack_params",
        [shape(8, CONVED, dtype=F32), shape(2, MINE, 128, dtype=F32)],
        [VMEM] * 5,
        (conv_weight, conv_bias[None], dt_bias[None], decay_rate[None], norm_gain[None]),
        scratch=[pltpu.VMEM((8, E), F32)],
        mb=12,
    )
    ub_other = call(hold, "hold", shape(LATE, 128), [VMEM] * 3, (ub_other, far, prm), mb=8)
    far_1, far_3 = along_x(far, 1), along_x(far, 3)
    ub_far = swap_diagonal(ub_other)
    halo, far_late = call(
        choose_halo, "choose_halo", [shape(HALO, D), shape(UNIT, 128)], [VMEM] * 3, (act, act_y, far), mb=8
    )
    halo = move(halo, halo_step)
    far_2 = along_x(far_late, 2)
    units = (ua, own_1, own_2, own_3, far, far_1, far_2, far_3)
    payload, late = call(
        pack_core,
        "pack_core",
        [shape(PAYLOAD, D), shape(2 * LATE, 128)],
        [VMEM] * 13,
        (act, act_y, halo, ub, ub_far, *units),
        mb=12,
    )
    swapped = swap_core(payload)
    late = (late, *[along_x(late, k) for k in (1, 2, 3)])
    scanned = [
        shape(SPAN, OWN),
        shape(SPAN, 2 * STATE),
        shape(MINE * GROUPS, GROUP, dtype=F32),
        shape(MINE * GROUPS, GROUP, dtype=F32),
        shape(GROUPS, STATE, OWN),
    ]
    *first, act, weight, given = call(
        first_scan,
        "first_scan",
        scanned + [shape(2, PAD, D), shape(WA, D), shape(STATE + HALO, OWN)],
        [VMEM] * 14,
        (act, act_y, halo, swapped, *units, prm, heads),
        scratch=[pltpu.VMEM((PAD, WA), F32)],
        mb=20,
        flops=1056 * D * WA,
        bytes_accessed=8 << 20,
    )
    *second, kept = call(
        second_scan,
        "second_scan",
        scanned + [shape(STATE + HALO, OWN)],
        [VMEM] * 4,
        (act, weight, prm, heads),
        scratch=[pltpu.VMEM((PAD, WA), F32)],
        mb=20,
        flops=16896 * D * WA,
        bytes_accessed=8 << 20,
    )
    mate = move(given, lambda z, yl, c, yh, x: dict(z=z ^ 1))
    pair = call(pair_state, "pair_state", shape(STATE + HALO, OWN), [VMEM] * 2, (kept, mate), mb=8)
    one, two, three = [move(pair, pair_step(m)) for m in (1, 2, 3)]
    earlier = (two, one, three)
    local, carry, maps = call(
        local_kernel,
        "local_kernel",
        [shape(2, SPAN, OWN, dtype=F32)] * 2 + [shape(2, SPAN, STATE)],
        [VMEM] * 11,
        (*first, *second, pair),
        mb=16,
        flops=8 * 1024 * D * OWN,
        bytes_accessed=16 << 20,
    )
    entered = call(earlier_pairs, "earlier_pairs", shape(STATE, OWN), [VMEM] * 3, earlier, mb=8)
    mate_entered = move(entered, lambda z, yl, c, yh, x: dict(z=z ^ 1))
    gate, weight = call(
        gate_kernel,
        "gate_kernel",
        [shape(2, SPAN, OWN, dtype=F32), shape(2, OWN, 512)],
        [VMEM] * (1 + len(late)),
        (act, *late),
        scratch=[pltpu.VMEM((OWN, D), BF16)],
        mb=16,
        flops=2 * 1024 * D * OWN,
        bytes_accessed=8 << 20,
    )
    half_out = [shape(2 * ROWS + HALO, D)] * 2
    half_scratch = [pltpu.VMEM((4, ROWS, OWN), BF16)]
    entering, keep, give = call(
        first_half,
        "first_half",
        [shape(2, STATE, OWN)] + half_out,
        [VMEM] * 9,
        (mate, entered, mate_entered, weight, prm, maps, local, carry, gate),
        scratch=half_scratch,
        mb=16,
        flops=1024 * D * OWN,
        bytes_accessed=4 << 20,
    )
    keep_2, give_2 = call(
        second_half,
        "second_half",
        half_out,
        [VMEM] * 7,
        (weight, entering, prm, maps, local, carry, gate),
        scratch=half_scratch,
        mb=16,
        flops=1024 * D * OWN,
        bytes_accessed=4 << 20,
    )
    part = call(
        pair_sum, "pair_sum", shape(2 * ROWS + HALO, D), [VMEM] * 3, (keep, swap_core(give), keep_2), mb=8
    )
    far_part = swap_y(part)
    out = call(
        last_kernel,
        "last_kernel",
        shape(ROWS, 2 * D),
        [VMEM] * 3,
        (keep_2, swap_core(give_2), far_part),
        scratch=[pltpu.VMEM((2, ROWS, D), BF16), pltpu.SemaphoreType.DMA((2,))],
        mb=8,
        out_specs=ANY,
    )
    return out[None]


def solution(mesh):
    placed = (
        P("fsdp", "seq", None),
        P("fsdp", "seq"),
        P(),
        P("fsdp", None),
        P(),
        P(),
        P(),
        P(),
        P(),
        P("fsdp", None),
    )
    return jax.shard_map(
        body, mesh=mesh, in_specs=placed, out_specs=P("fsdp", "seq", None), check_vma=False
    )
```
